512 devices in a mesh: role: 2 (over core), grp: 64 (over x, z), tp: 4 (over y).
Axes of the slice: x: 4, y: 4, z: 16, core: 2. Of those that a mesh axis runs over, the one named last changes fastest.
Arguments:
- queries: bfloat16 [512, 64, 576], P(('role', 'grp', 'tp')), may hold values from -50 to 50
- latent_cache: bfloat16 [512, 384, 576], P(('role', 'grp', 'tp')), may hold values from -6 to 6
- lengths: int32 [512], P(('role', 'grp', 'tp')), may hold values from 2 to 384, as said below
- value_up: bfloat16 [64, 512, 128], P(('role', 'tp')), may hold values from -0.25 to 0.25
- output_weight: bfloat16 [3584, 8192], P('grp', ('role', 'tp')), may hold values from -0.0625 to 0.0625
- residual: bfloat16 [3584, 512], P('grp'), may hold values from -15 to 15
- norm_gain: float32 [3584], replicated, may hold values from 0.5 to 1.5
- routed_experts: int32 [512, 8], replicated, may hold values from 0 to 63, as said below
- route_weights: float32 [512, 8], replicated, may hold values from 0.1 to 0.6
- gate_weight: bfloat16 [64, 3584, 1024], P('grp', None, ('role', 'tp')), may hold values from -0.09375 to 0.09375
- up_weight: bfloat16 [64, 3584, 1024], P('grp', None, ('role', 'tp')), may hold values from -0.09375 to 0.09375
- down_weight: bfloat16 [64, 1024, 3584], P('grp', ('role', 'tp')), may hold values from -0.1875 to 0.1875
Outputs:
- layer_output: bfloat16 [3584, 512], P('grp', ('role', 'tp'))
The draws below stay inside these ranges and needn't reach their ends.
Inputs may be any that keep to these rules, and one draw needn't show every extreme that they name: `routed_experts`: each row names 8 different experts. In each aligned block of 64 rows no expert is named by more than 16 rows, and one expert, the same in every block, is named by exactly 16 rows of each block. `lengths`: at least one request has length 384.
All inputs are finite; a program needn't handle non-finite values.
Results may differ from the reference program's by a relative error of at most 0.028.
Values may be sent and summed in bfloat16 or wider, within the bound.
No kernel may reach another device: no remote copies, remote signals or barrier semaphores. Data moves between devices by JAX's collectives and lax.ppermute only.
A program may use at most 64 MiB of HBM per device.

```python
import math
import jax
import jax.numpy as jnp
from jax import lax

D = 3584
HEADS = 64
LAT = 512
VD = 128
HID = 1024
CTX = 384
QK = 576
EXPERTS = 64
TOPK = 8
TOKENS = 512
ROWBLK = 64
MOST = 16
CAP = 128
N_ROLE = 2
N_TP = 4


def draw_queries(key, part):
    key = jax.random.fold_in(key, 1)
    return jnp.clip(jax.random.normal(key, (TOKENS, HEADS, QK), jnp.float32), -6.0, 6.0).astype(jnp.bfloat16)


def draw_latent_cache(key, part):
    key = jax.random.fold_in(key, 2)
    return jnp.clip(jax.random.normal(key, (TOKENS, CTX, QK), jnp.float32), -6.0, 6.0).astype(jnp.bfloat16)


def draw_lengths(key, part):
    key = jax.random.fold_in(key, 3)
    length_key, place_key = jax.random.split(key)
    drawn = jax.random.randint(length_key, (TOKENS,), 2, CTX + 1)
    longest = jax.random.randint(place_key, (), 0, TOKENS)
    return jnp.where(jnp.arange(TOKENS) == longest, CTX, drawn).astype(jnp.int32)


def draw_residual(key, part):
    key = jax.random.fold_in(key, 4)
    token_key, value_key = jax.random.split(key)
    rising = jnp.arange(D, dtype=jnp.float32)[:, None] / D
    token_scale = jnp.exp(jax.random.uniform(token_key, (1, TOKENS), jnp.float32, math.log(0.25), math.log(2.5)))
    values = jnp.clip(jax.random.normal(value_key, (D, TOKENS), jnp.float32), -6.0, 6.0)
    return (values * token_scale * 0.1 * jnp.exp(rising * math.log(10.0))).astype(jnp.bfloat16)


def draw_routed_experts(key, part):
    key = jax.random.fold_in(key, 5)
    hot_key, order_key, shuffle_key = jax.random.split(key, 3)
    block_total = TOKENS // ROWBLK
    windows = EXPERTS // TOPK
    hot_expert = jax.random.randint(hot_key, (), 0, EXPERTS)
    orderings = jax.vmap(lambda subkey: jax.random.permutation(subkey, EXPERTS))(jax.random.split(order_key, block_total))
    places = jnp.arange(EXPERTS)[None, :]
    orderings = jnp.where(places == 0, hot_expert, jnp.where(orderings == hot_expert, orderings[:, :1], orderings))
    row_ids = jnp.arange(ROWBLK)[:, None]
    slot_ids = jnp.arange(TOPK)[None, :]
    window_index = (row_ids * TOPK + slot_ids) % EXPERTS
    window_index = jnp.where((row_ids % windows == 1) & (slot_ids == TOPK - 1), 0, window_index)
    shuffles = jax.vmap(lambda subkey: jax.random.permutation(subkey, ROWBLK))(jax.random.split(shuffle_key, block_total))
    block_index = window_index[shuffles]
    chosen = jax.vmap(lambda ordering, indices: ordering[indices])(orderings, block_index)
    return chosen.reshape(TOKENS, TOPK).astype(jnp.int32)


def block_scale(rng, dims, cuts, least, high):
    def one(position, shards_of):
        heights = jax.random.uniform(jax.random.fold_in(jax.random.fold_in(rng, 6), position), (shards_of,), jnp.float32, least / len(cuts), high / len(cuts))
        return jnp.repeat(jnp.exp(heights), dims[position] // shards_of).reshape((-1,) + (1,) * (len(dims) - position - 1))

    gain = one(*cuts[0])
    for cut in cuts[1:]:
        gain = gain * one(*cut)
    return gain


def gaussian(rng, extent, deviation, limit, cuts=(), held_as=jnp.bfloat16):
    values = deviation * jax.random.normal(rng, extent, jnp.float32)
    if cuts:
        values = values * block_scale(rng, extent, cuts, -0.22, 0.18)
    return jnp.clip(values, -limit, limit).astype(held_as)


def setup_inputs(seed: int = 0) -> dict:
    seeds = jax.random.split(jax.random.key(seed), 13)
    return {
        "queries": draw_queries(jax.random.fold_in(seeds[12], 71), 0),
        "latent_cache": draw_latent_cache(jax.random.fold_in(seeds[12], 71), 0),
        "lengths": draw_lengths(jax.random.fold_in(seeds[12], 71), 0),
        "value_up": gaussian(seeds[3], (HEADS, LAT, VD), LAT ** -0.5, 0.25, ((0, 8),)),
        "output_weight": gaussian(seeds[4], (D, HEADS * VD), (HEADS * VD) ** -0.5, 0.0625, ((0, 64), (1, 8))),
        "residual": draw_residual(jax.random.fold_in(seeds[12], 71), 0),
        "norm_gain": jnp.clip(1.0 + 0.1 * jax.random.normal(seeds[6], (D,), jnp.float32), 0.5, 1.5),
        "routed_experts": draw_routed_experts(jax.random.fold_in(seeds[12], 71), 0),
        "route_weights": jnp.clip(jax.random.uniform(seeds[8], (TOKENS, TOPK), jnp.float32, 0.1, 0.6), 0.1, 0.6),
        "gate_weight": gaussian(seeds[9], (EXPERTS, D, HID), D ** -0.5, 0.09375, ((0, 64), (2, 8))),
        "up_weight": gaussian(seeds[10], (EXPERTS, D, HID), D ** -0.5, 0.09375, ((0, 64), (2, 8))),
        "down_weight": gaussian(seeds[11], (EXPERTS, HID, D), HID ** -0.5, 0.1875, ((0, 64), (1, 8))),
    }


SOFTMAX_SCALE = 192.0 ** (-0.5)
NORM_EPS = 1e-06

def attend_block(block):
    query_rows, cache_rows, length_rows = block
    query_float = query_rows.astype(jnp.float32)
    cache_float = cache_rows.astype(jnp.float32)
    scores = jnp.einsum('thc,tjc->thj', query_float, cache_float, precision=lax.Precision.HIGHEST) * SOFTMAX_SCALE
    places = jnp.arange(cache_rows.shape[1], dtype=jnp.int32)
    visible = (places[None, :] < length_rows[:, None])[:, None, :]
    row_max = lax.optimization_barrier(jnp.max(jnp.where(visible, scores, -1e+30), axis=2, keepdims=True))
    weights = jnp.where(visible, jnp.exp(scores - row_max), 0.0)
    row_total = lax.optimization_barrier(jnp.sum(weights, axis=2, keepdims=True))
    rounded = lax.optimization_barrier(weights.astype(jnp.bfloat16)).astype(jnp.float32)
    summed = jnp.einsum('thj,tjc->thc', rounded, cache_float[:, :, :LAT], precision=lax.Precision.HIGHEST)
    return (summed / row_total).astype(jnp.bfloat16)

def reference(queries, latent_cache, lengths, value_up, output_weight, residual, norm_gain, routed_experts, route_weights, gate_weight, up_weight, down_weight):
    block_size = math.gcd(TOKENS, 32)
    block_count = TOKENS // block_size
    attended = lax.map(attend_block, (queries.reshape(block_count, block_size, HEADS, QK), latent_cache.reshape(block_count, block_size, CTX, QK), lengths.reshape(block_count, block_size)))
    attended = attended.reshape(TOKENS, HEADS, LAT)
    head_values = jnp.einsum('thc,hcv->thv', attended.astype(jnp.float32), value_up.astype(jnp.float32), precision=lax.Precision.HIGHEST)
    head_values = head_values.astype(jnp.bfloat16).reshape(TOKENS, HEADS * VD)
    attention_out = jnp.dot(output_weight, head_values.T, preferred_element_type=jnp.float32)
    hidden_state = (residual.astype(jnp.float32) + attention_out).astype(jnp.bfloat16)
    hidden_float = hidden_state.astype(jnp.float32)
    mean_square = lax.optimization_barrier(jnp.mean(hidden_float * hidden_float, axis=0))
    normed = (hidden_float * lax.rsqrt(mean_square + NORM_EPS)[None, :] * norm_gain[:, None]).astype(jnp.bfloat16)
    token_rows = normed.T
    block_total = TOKENS // ROWBLK
    matches = routed_experts[:, :, None] == jnp.arange(EXPERTS, dtype=jnp.int32)[None, None, :]
    named_count = lax.optimization_barrier(jnp.sum(matches.astype(jnp.int32), axis=1)).reshape(block_total, ROWBLK, EXPERTS)
    slot_rank = jnp.cumsum(named_count, axis=1) - named_count
    in_slot = (named_count[:, :, :, None] == 1) & (slot_rank[:, :, :, None] == jnp.arange(MOST, dtype=jnp.int32))
    token_index = jnp.arange(TOKENS, dtype=jnp.int32).reshape(block_total, ROWBLK)
    source = lax.optimization_barrier(jnp.sum(jnp.where(in_slot, token_index[:, :, None, None], 0), axis=1)).astype(jnp.int32)
    filled = jnp.any(in_slot, axis=1)
    source = jnp.transpose(source, (1, 0, 2)).reshape(EXPERTS, CAP)
    filled = jnp.transpose(filled, (1, 0, 2)).reshape(EXPERTS, CAP)
    hid_blocks = N_ROLE * N_TP
    hid_size = HID // hid_blocks

    def run_expert(args):
        slot_table, present, gate_matrix, up_matrix, down_matrix = args
        picked = jnp.where(present[:, None], token_rows[slot_table], jnp.zeros((), token_rows.dtype))
        gate_part = jnp.dot(picked, gate_matrix, preferred_element_type=jnp.float32)
        up_part = jnp.dot(picked, up_matrix, preferred_element_type=jnp.float32)
        activated = (jax.nn.silu(gate_part) * up_part).astype(jnp.bfloat16)
        act_blocks = activated.reshape(CAP, hid_blocks, hid_size).astype(jnp.float32)
        down_blocks = down_matrix.reshape(hid_blocks, hid_size, D).astype(jnp.float32)
        partials = jnp.einsum('cbh,bhd->bcd', act_blocks, down_blocks, precision=lax.Precision.HIGHEST)
        partials = lax.optimization_barrier(partials.astype(jnp.bfloat16)).astype(jnp.float32)
        return lax.optimization_barrier(jnp.sum(partials, axis=0)).astype(jnp.bfloat16)
    expert_out = lax.map(run_expert, (source, filled, gate_weight, up_weight, down_weight))
    token_rank = jnp.take_along_axis(slot_rank.reshape(TOKENS, EXPERTS), routed_experts, axis=1)
    slot_index = (jnp.arange(TOKENS, dtype=jnp.int32) // ROWBLK)[:, None] * MOST + token_rank
    gathered = expert_out[routed_experts, slot_index].astype(jnp.float32)
    mixture = lax.optimization_barrier(jnp.sum(route_weights[:, :, None] * gathered, axis=1))
    return (hidden_float + mixture.T).astype(jnp.bfloat16)
```

```python
import jax
import jax.numpy as jnp
from jax import lax
from jax.experimental import pallas as pl
from jax.experimental.pallas import tpu as pltpu
from jax.sharding import Mesh
from jax.sharding import PartitionSpec as P

LAT = 512
SOFTMAX_SCALE = 192.0 ** (-0.5)
NORM_EPS = 1e-06

ROLE, X, ZH, ZL, TP = 2, 4, 4, 4, 4
Z = ZH * ZL
MEMBERS = ROLE * TP
ROWBLK = 64
MOST = 16
EXPERTS = 64
COLS = 56
WIDTH = 3584
PART = ZH * COLS
PLANE = Z * COLS
HALF = 64

F32 = jnp.float32
BF16 = jnp.bfloat16
VMEM_LIMIT = 48 * 1024 * 1024


def nt_dot(a, b):
    return lax.dot_general(a, b, (((1,), (1,)), ((), ())), preferred_element_type=F32)


def nn_dot(a, b):
    return lax.dot_general(a, b, (((1,), (0,)), ((), ())), preferred_element_type=F32)


def local_call(body, out_shape, *args, scratch=(), smem=()):
    specs = [
        pl.BlockSpec(memory_space=pltpu.SMEM if i in smem else pltpu.VMEM)
        for i in range(len(args))
    ]
    return pl.pallas_call(
        body,
        out_shape=out_shape,
        in_specs=specs,
        out_specs=jax.tree.map(lambda _: pl.BlockSpec(memory_space=pltpu.VMEM), out_shape),
        scratch_shapes=list(scratch),
        compiler_params=pltpu.CompilerParams(vmem_limit_bytes=VMEM_LIMIT),
    )(*args)


def shape(dims, dtype=BF16):
    return jax.ShapeDtypeStruct(dims, dtype)


def attend_kernel(length_ref, query_ref, cache_ref, out_ref):
    cache = cache_ref[0]
    scores = nt_dot(query_ref[0], cache) * SOFTMAX_SCALE
    visible = lax.broadcasted_iota(jnp.int32, scores.shape, 1) < length_ref[0]
    scores = jnp.where(visible, scores, -1e30)
    row_max = jnp.max(scores, axis=1, keepdims=True)
    weights = jnp.where(visible, jnp.exp(scores - row_max), 0.0)
    row_total = jnp.sum(weights, axis=1, keepdims=True)
    summed = nn_dot(weights.astype(BF16), cache[:, :LAT])
    out_ref[...] = (summed / row_total).astype(BF16)


def value_kernel(att_ref, value_ref, out_ref):
    heads = value_ref.shape[0]
    att = att_ref[...]
    rows = att.shape[0]
    row_head = lax.broadcasted_iota(jnp.int32, (rows, 128), 0) % heads
    for head in range(heads):
        product = nn_dot(att, value_ref[head])
        kept = jnp.where(row_head == head, product, 0.0)
        value = jnp.sum(kept.reshape(rows // heads, heads, 128), axis=1).astype(BF16)
        out_ref[:, :, head * 128 : (head + 1) * 128] = jnp.broadcast_to(
            value[None], (out_ref.shape[0],) + value.shape
        )


def project_kernel(values_ref, weight_ref, out_ref):
    rows = values_ref.shape[0]
    place = lax.broadcasted_iota(jnp.int32, (rows, rows), 0)
    source = lax.broadcasted_iota(jnp.int32, (rows, rows), 1)
    lane = place % TP
    chunk = (place // TP) % (X * ZL)
    role = place // (TP * X * ZL)
    order = (source == chunk * MEMBERS + role * TP + lane).astype(F32).astype(BF16)
    values = nn_dot(order, values_ref[...]).astype(BF16)
    out_ref[...] = nt_dot(values, weight_ref[...]).astype(BF16)


def reduce_kernel(parts_ref, out_ref):
    total = jnp.sum(parts_ref[...].astype(F32), axis=0).astype(BF16)
    out_ref[...] = jnp.broadcast_to(total[None], out_ref.shape)


def route_kernel(
    place_ref, routed_ref, weight_ref, pick_ref, high_ref, low_ref, named_ref, rank_ref
):
    dims = (EXPERTS, ROWBLK)
    expert_ids = lax.broadcasted_iota(jnp.int32, dims, 0)
    named = jnp.zeros(dims, F32)
    weights = jnp.zeros(dims, F32)
    for k in range(routed_ref.shape[0]):
        chosen = expert_ids == routed_ref[k : k + 1, :]
        named = named + jnp.where(chosen, 1.0, 0.0)
        weights = weights + jnp.where(chosen, weight_ref[k : k + 1, :], 0.0)
    earlier = lax.broadcasted_iota(jnp.int32, (ROWBLK, ROWBLK), 0) < lax.broadcasted_iota(
        jnp.int32, (ROWBLK, ROWBLK), 1
    )
    before = jnp.where(earlier, 1.0, 0.0).astype(BF16)
    rank = nn_dot(named.astype(BF16), before)
    rank = jnp.where(named > 0.5, rank, -1.0)
    rank_ref[...] = rank
    named_ref[...] = weights
    slots = lax.broadcasted_iota(jnp.int32, (MOST, ROWBLK), 0).astype(F32)
    for half in range(2):
        for z in range(Z):
            for pair in range(2):
                expert = (half * 2 + pair) * Z + z
                hit = rank_ref[expert : expert + 1, :] == slots
                table = jnp.where(hit, named_ref[expert : expert + 1, :], 0.0)
                high = table.astype(BF16)
                low = (table - high.astype(F32)).astype(BF16)
                rows = pl.ds(z * 32 + pair * MOST, MOST)
                lanes = pl.ds(half * HALF, ROWBLK)
                high_ref[rows, lanes] = high
                low_ref[rows, lanes] = low
    for x in range(X):
        row = rank_ref[pl.ds(x * Z + place_ref[0] * ZL + place_ref[1], 1), :]
        pick_ref[x * MOST : (x + 1) * MOST, :] = jnp.where(row == slots, 1.0, 0.0).astype(BF16)


def dispatch_kernel(place_ref, parts_ref, residual_ref, pick_ref, out_ref, own_ref):
    pick = pick_ref[...]
    own = jnp.zeros((COLS, ROWBLK), F32)
    column = lax.broadcasted_iota(jnp.int32, (COLS, PART), 0)
    feature = lax.broadcasted_iota(jnp.int32, (COLS, PART), 1)
    for zl in range(ZL):
        attention = jnp.concatenate(
            [parts_ref[zh * ZL + zl].astype(F32) for zh in range(ZH)], axis=0
        )
        hidden = (residual_ref[zl].astype(F32) + attention).astype(BF16)
        wanted = (feature == column + place_ref[0] * COLS) & (place_ref[1] == zl)
        own = own + nt_dot(jnp.where(wanted, 1.0, 0.0).astype(BF16), hidden)
        rows = nn_dot(pick, hidden).astype(BF16)
        for x in range(X):
            piece = rows[x * MOST : (x + 1) * MOST]
            for lane in range(TP):
                out_ref[x * TP + lane, zl] = piece
    own_ref[...] = own


def expert_kernel(
    arrived_ref, gain_ref, own_in_ref, peer_in_ref, own_down_ref, peer_down_ref, out_ref
):
    rows = TP * MOST
    values = []
    total = jnp.zeros((rows, 1), F32)
    for x in range(X):
        for zl in range(ZL):
            value = jnp.concatenate(
                [arrived_ref[x * TP + lane, zl] for lane in range(TP)], axis=0
            ).astype(F32)
            total = total + jnp.sum(value * value, axis=1, keepdims=True)
            values.append(value)
    inverse = lax.rsqrt(total / WIDTH + NORM_EPS)
    own = jnp.zeros((rows, 256), F32)
    peer = jnp.zeros((rows, 256), F32)
    for i, value in enumerate(values):
        normed = (value * inverse * gain_ref[i]).astype(BF16)
        own = own + nn_dot(normed, own_in_ref[i])
        peer = peer + nn_dot(normed, peer_in_ref[i])

    def activate(both):
        gate, up = both[:, :128], both[:, 128:]
        return (gate / (1.0 + jnp.exp(-gate)) * up).astype(BF16)

    own_act, peer_act = activate(own), activate(peer)
    for x in range(X):
        lanes = pl.ds(x * PLANE, PLANE)
        product = nn_dot(own_act, own_down_ref[:, lanes]) + nn_dot(
            peer_act, peer_down_ref[:, lanes]
        )
        product = product.astype(BF16)
        for lane in range(TP):
            out_ref[x * TP + lane] = product[lane * MOST : (lane + 1) * MOST]


def columns_kernel(parts_ref, out_ref):
    summed = []
    for x in range(X):
        total = parts_ref[x * TP].astype(F32)
        for lane in range(1, TP):
            total = total + parts_ref[x * TP + lane].astype(F32)
        summed.append(total)
    low = jnp.concatenate(summed[:2], axis=0)
    high = jnp.concatenate(summed[2:], axis=0)
    gap = jnp.zeros((32, HALF - COLS), F32)
    for z in range(Z):
        cut = slice(z * COLS, (z + 1) * COLS)
        out_ref[z] = jnp.concatenate([low[:, cut], gap, high[:, cut], gap], axis=1).astype(BF16)


def combine_kernel(returned_ref, high_ref, low_ref, own_ref, out_ref):
    returned = returned_ref[...]
    dims = (((0,), (0,)), ((), ()))
    mixed = lax.dot_general(returned, high_ref[...], dims, preferred_element_type=F32)
    mixed = mixed + lax.dot_general(returned, low_ref[...], dims, preferred_element_type=F32)
    mixture = mixed[:COLS, :ROWBLK] + mixed[HALF : HALF + COLS, HALF : HALF + ROWBLK]
    out_ref[...] = (own_ref[...] + mixture).astype(BF16)


def shards(
    queries,
    latent_cache,
    lengths,
    value_up,
    output_weight,
    residual,
    norm_gain,
    routed_experts,
    route_weights,
    gate_weight,
    up_weight,
    down_weight,
):
    swap = [(0, 1), (1, 0)]
    block = lax.axis_index("role") * TP + lax.axis_index("tp")
    place = jnp.stack([lax.axis_index("zh"), lax.axis_index("zl")]).astype(jnp.int32)

    weight_rows = lax.all_gather(output_weight, "zh", axis=0, tiled=True)
    residual_block = lax.dynamic_slice_in_dim(residual, block * ROWBLK, ROWBLK, 1).T
    residual_rows = lax.all_gather(residual_block, ("zh", "zl"), axis=0, tiled=False)
    residual_rows = (
        residual_rows.reshape(ZH, ZL, ROWBLK, COLS)
        .transpose(1, 2, 0, 3)
        .reshape(ZL, ROWBLK, PART)
    )
    gain_rows = norm_gain.reshape(X, ZH, ZL, COLS).transpose(0, 2, 1, 3).reshape(X * ZL, 1, PART)
    own_in = jnp.concatenate([gate_weight[0], up_weight[0]], axis=1)
    own_in = (
        own_in.reshape(X, ZH, ZL, COLS, 256).transpose(0, 2, 1, 3, 4).reshape(X * ZL, PART, 256)
    )
    own_down = down_weight[0]
    peer_in = lax.ppermute(own_in, "role", swap)
    peer_down = lax.ppermute(own_down, "role", swap)
    routed_rows = lax.dynamic_slice_in_dim(routed_experts, block * ROWBLK, ROWBLK, 0).T
    route_rows = lax.dynamic_slice_in_dim(route_weights, block * ROWBLK, ROWBLK, 0).T
    pick, high, low = local_call(
        route_kernel,
        (shape((X * MOST, ROWBLK)), shape((Z * 32, 128)), shape((Z * 32, 128))),
        place,
        routed_rows,
        route_rows,
        scratch=(pltpu.VMEM((EXPERTS, ROWBLK), F32), pltpu.VMEM((EXPERTS, ROWBLK), F32)),
        smem=(0,),
    )

    heads = queries.shape[1]
    own_heads = heads // MEMBERS
    attended = local_call(
        attend_kernel, shape((heads, LAT)), lengths, queries, latent_cache, smem=(0,)
    )
    attended = attended.reshape(MEMBERS, own_heads, LAT)
    regrouped = lax.all_to_all(attended, ("role", "tp"), 0, 0, tiled=True)
    values = local_call(
        value_kernel,
        shape((X * ZL, MEMBERS, own_heads * 128)),
        regrouped.reshape(MEMBERS * own_heads, LAT),
        value_up,
    )
    gathered = lax.all_to_all(values, ("x", "zl"), 0, 0, tiled=True)
    projected = local_call(
        project_kernel,
        shape((X * ZL * MEMBERS, PART)),
        gathered.reshape(X * ZL * MEMBERS, own_heads * 128),
        weight_rows,
    )
    head_parts = lax.all_to_all(
        projected.reshape(MEMBERS, ZL * TP, PART), ("role", "tp"), 0, 0, tiled=True
    )
    attention = local_call(reduce_kernel, shape((Z, ZL * TP, PART)), head_parts)
    attention = lax.all_to_all(attention, ("zh", "zl"), 0, 0, tiled=True)
    outbound, own_hidden = local_call(
        dispatch_kernel,
        (shape((X * TP, ZL, MOST, PART)), shape((COLS, ROWBLK), F32)),
        place,
        attention,
        residual_rows,
        pick,
        smem=(0,),
    )
    arrived = lax.all_to_all(outbound, ("x", "tp"), 0, 0, tiled=True)
    partial = local_call(
        expert_kernel,
        shape((X * TP, MOST, PLANE)),
        arrived,
        gain_rows,
        own_in,
        peer_in,
        own_down,
        peer_down,
    )
    hidden_parts = lax.all_to_all(partial, ("x", "tp"), 0, 0, tiled=True)
    columns = local_call(columns_kernel, shape((Z, 32, 128)), hidden_parts)
    returned = lax.all_to_all(columns, ("zh", "zl"), 0, 0, tiled=True)
    return local_call(
        combine_kernel,
        shape((COLS, ROWBLK)),
        returned.reshape(Z * 32, 128),
        high,
        low,
        own_hidden,
    )


def solution(mesh):
    grp = ("x", "zh", "zl")
    fine = Mesh(
        mesh.devices.reshape(ROLE, X, ZH, ZL, TP), ("role", "x", "zh", "zl", "tp")
    )
    return jax.shard_map(
        shards,
        mesh=fine,
        in_specs=(
            P(("role",) + grp + ("tp",), None, None),
            P(("role",) + grp + ("tp",), None, None),
            P(("role",) + grp + ("tp",)),
            P(("role", "tp"), None, None),
            P(grp, ("role", "tp")),
            P(grp, None),
            P(),
            P(),
            P(),
            P(grp, None, ("role", "tp")),
            P(grp, None, ("role", "tp")),
            P(grp, ("role", "tp"), None),
        ),
        out_specs=P(grp, ("role", "tp")),
        check_vma=False,
    )
```

```python
import jax
import jax.numpy as jnp
from jax import lax
from jax.experimental import pallas as pl
from jax.experimental.pallas import tpu as pltpu
from jax.sharding import Mesh
from jax.sharding import PartitionSpec as P

LAT = 512
SOFTMAX_SCALE = 192.0 ** (-0.5)
NORM_EPS = 1e-06

ROLE, X, ZH, ZL, TP = 2, 4, 4, 4, 4
Z = ZH * ZL
MEMBERS = ROLE * TP
ROWBLK = 64
MOST = 16
EXPERTS = 64
COLS = 56
WIDTH = 3584
PART = ZH * COLS
PLANE = Z * COLS
HALF = 64

F32 = jnp.float32
BF16 = jnp.bfloat16
VMEM_LIMIT = 48 * 1024 * 1024


def nt_dot(a, b):
    return lax.dot_general(a, b, (((1,), (1,)), ((), ())), preferred_element_type=F32)


def nn_dot(a, b):
    return lax.dot_general(a, b, (((1,), (0,)), ((), ())), preferred_element_type=F32)


def local_call(body, out_shape, *args, scratch=(), smem=()):
    specs = [
        pl.BlockSpec(memory_space=pltpu.SMEM if i in smem else pltpu.VMEM)
        for i in range(len(args))
    ]
    return pl.pallas_call(
        body,
        out_shape=out_shape,
        in_specs=specs,
        out_specs=jax.tree.map(lambda _: pl.BlockSpec(memory_space=pltpu.VMEM), out_shape),
        scratch_shapes=list(scratch),
        compiler_params=pltpu.CompilerParams(vmem_limit_bytes=VMEM_LIMIT),
    )(*args)


def shape(dims, dtype=BF16):
    return jax.ShapeDtypeStruct(dims, dtype)


def attend_kernel(length_ref, query_ref, cache_ref, out_ref):
    cache = cache_ref[0]
    scores = nn_dot(query_ref[0], cache) * SOFTMAX_SCALE
    visible = lax.broadcasted_iota(jnp.int32, scores.shape, 1) < length_ref[0]
    scores = jnp.where(visible, scores, -1e30)
    row_max = jnp.max(scores, axis=1, keepdims=True)
    weights = jnp.where(visible, jnp.exp(scores - row_max), 0.0)
    row_total = jnp.sum(weights, axis=1, keepdims=True)
    summed = nt_dot(weights.astype(BF16), cache[:LAT])
    out_ref[...] = (summed / row_total).astype(BF16)


def value_kernel(att_ref, value_ref, out_ref):
    heads = value_ref.shape[0]
    att = att_ref[...]
    rows = att.shape[0]
    row_head = lax.broadcasted_iota(jnp.int32, (rows, 128), 0) % heads
    for head in range(heads):
        product = nn_dot(att, value_ref[head])
        kept = jnp.where(row_head == head, product, 0.0)
        value = jnp.sum(kept.reshape(rows // heads, heads, 128), axis=1).astype(BF16)
        out_ref[:, :, head * 128 : (head + 1) * 128] = jnp.broadcast_to(
            value[None], (out_ref.shape[0],) + value.shape
        )


def project_kernel(place_ref, values_ref, *refs):
    payloads, (out_ref, residual_ref, held_ref) = refs[:ZH], refs[ZH:]
    zh = place_ref[0]
    for step, payload in enumerate(payloads):
        held_ref[lax.rem(zh + ZH - step, ZH)] = payload[...]
    rows = values_ref.shape[0]
    place = lax.broadcasted_iota(jnp.int32, (rows, rows), 0)
    source = lax.broadcasted_iota(jnp.int32, (rows, rows), 1)
    lane = place % TP
    chunk = (place // TP) % (X * ZL)
    role = place // (TP * X * ZL)
    order = (source == chunk * MEMBERS + role * TP + lane).astype(F32).astype(BF16)
    values = nn_dot(order, values_ref[...]).astype(BF16)
    depth = values.shape[1]
    token = lax.broadcasted_iota(jnp.int32, (ZL * TP, ROWBLK), 0)
    request = lax.broadcasted_iota(jnp.int32, (ZL * TP, ROWBLK), 1)
    mine = (request == token + zh * (ZL * TP)).astype(F32).astype(BF16)
    out, residual = [], []
    for i in range(ZH):
        held = held_ref[i]
        out.append(nt_dot(values, held[:, :depth]))
        residual.append(nt_dot(mine, held[:, depth : depth + ROWBLK]))
    out_ref[...] = jnp.concatenate(out, axis=1).astype(BF16)
    residual_ref[...] = jnp.concatenate(residual, axis=1)


def hidden_kernel(parts_ref, residual_ref, out_ref):
    total = jnp.sum(parts_ref[...].astype(F32), axis=0)
    total = (residual_ref[...] + total).astype(BF16)
    out_ref[...] = jnp.broadcast_to(total[None], out_ref.shape)


def route_kernel(
    place_ref, routed_ref, weight_ref, pick_ref, high_ref, low_ref, named_ref, rank_ref
):
    dims = (EXPERTS, ROWBLK)
    expert_ids = lax.broadcasted_iota(jnp.int32, dims, 0)
    named = jnp.zeros(dims, F32)
    weights = jnp.zeros(dims, F32)
    for k in range(routed_ref.shape[0]):
        chosen = expert_ids == routed_ref[k : k + 1, :]
        named = named + jnp.where(chosen, 1.0, 0.0)
        weights = weights + jnp.where(chosen, weight_ref[k : k + 1, :], 0.0)
    earlier = lax.broadcasted_iota(jnp.int32, (ROWBLK, ROWBLK), 0) < lax.broadcasted_iota(
        jnp.int32, (ROWBLK, ROWBLK), 1
    )
    before = jnp.where(earlier, 1.0, 0.0).astype(BF16)
    rank = nn_dot(named.astype(BF16), before)
    rank = jnp.where(named > 0.5, rank, -1.0)
    rank_ref[...] = rank
    named_ref[...] = weights
    slots = lax.broadcasted_iota(jnp.int32, (MOST, ROWBLK), 0).astype(F32)
    for half in range(2):
        for z in range(Z):
            for pair in range(2):
                expert = (half * 2 + pair) * Z + z
                hit = rank_ref[expert : expert + 1, :] == slots
                table = jnp.where(hit, named_ref[expert : expert + 1, :], 0.0)
                high = table.astype(BF16)
                low = (table - high.astype(F32)).astype(BF16)
                rows = pl.ds(z * 32 + pair * MOST, MOST)
                lanes = pl.ds(half * HALF, ROWBLK)
                high_ref[rows, lanes] = high
                low_ref[rows, lanes] = low
    for x in range(X):
        row = rank_ref[pl.ds(x * Z + place_ref[0] * ZL + place_ref[1], 1), :]
        pick_ref[x * MOST : (x + 1) * MOST, :] = jnp.where(row == slots, 1.0, 0.0).astype(BF16)


def dispatch_kernel(place_ref, parts_ref, pick_ref, out_ref, own_ref):
    hidden = jnp.concatenate(
        [
            jnp.concatenate([parts_ref[zh * ZL + zl].astype(F32) for zh in range(ZH)], axis=0)
            for zl in range(ZL)
        ],
        axis=1,
    ).astype(BF16)
    rows = nn_dot(pick_ref[...], hidden).astype(BF16)
    for x in range(X):
        piece = rows[x * MOST : (x + 1) * MOST]
        for lane in range(TP):
            out_ref[x * TP + lane] = piece
    column = lax.broadcasted_iota(jnp.int32, (COLS, PLANE), 0)
    feature = lax.broadcasted_iota(jnp.int32, (COLS, PLANE), 1)
    wanted = feature == column + (place_ref[1] * PART + place_ref[0] * COLS)
    own_ref[...] = nt_dot(jnp.where(wanted, 1.0, 0.0).astype(BF16), hidden)


def expert_kernel(
    arrived_ref, gain_ref, own_in_ref, peer_in_ref, own_down_ref, peer_down_ref, out_ref
):
    rows = TP * MOST
    values = []
    total = jnp.zeros((rows, 1), F32)
    for x in range(X):
        value = jnp.concatenate(
            [arrived_ref[x * TP + lane] for lane in range(TP)], axis=0
        ).astype(F32)
        total = total + jnp.sum(value * value, axis=1, keepdims=True)
        values.append(value)
    inverse = lax.rsqrt(total / WIDTH + NORM_EPS)
    own = jnp.zeros((rows, 256), F32)
    peer = jnp.zeros((rows, 256), F32)
    for i, value in enumerate(values):
        normed = (value * inverse * gain_ref[i]).astype(BF16)
        own = own + nn_dot(normed, own_in_ref[i])
        peer = peer + nn_dot(normed, peer_in_ref[i])

    def activate(both):
        gate, up = both[:, :128], both[:, 128:]
        return (gate / (1.0 + jnp.exp(-gate)) * up).astype(BF16)

    own_act, peer_act = activate(own), activate(peer)
    for x in range(X):
        lanes = pl.ds(x * PLANE, PLANE)
        product = nn_dot(own_act, own_down_ref[:, lanes]) + nn_dot(
            peer_act, peer_down_ref[:, lanes]
        )
        product = product.astype(BF16)
        for lane in range(TP):
            out_ref[x * TP + lane] = product[lane * MOST : (lane + 1) * MOST]


def columns_kernel(parts_ref, out_ref):
    summed = []
    for x in range(X):
        total = parts_ref[x * TP].astype(F32)
        for lane in range(1, TP):
            total = total + parts_ref[x * TP + lane].astype(F32)
        summed.append(total)
    low = jnp.concatenate(summed[:2], axis=0)
    high = jnp.concatenate(summed[2:], axis=0)
    gap = jnp.zeros((32, HALF - COLS), F32)
    for z in range(Z):
        cut = slice(z * COLS, (z + 1) * COLS)
        out_ref[z] = jnp.concatenate([low[:, cut], gap, high[:, cut], gap], axis=1).astype(BF16)


def combine_kernel(returned_ref, high_ref, low_ref, own_ref, out_ref):
    returned = returned_ref[...]
    dims = (((0,), (0,)), ((), ()))
    mixed = lax.dot_general(returned, high_ref[...], dims, preferred_element_type=F32)
    mixed = mixed + lax.dot_general(returned, low_ref[...], dims, preferred_element_type=F32)
    mixture = mixed[:COLS, :ROWBLK] + mixed[HALF : HALF + COLS, HALF : HALF + ROWBLK]
    out_ref[...] = (own_ref[...] + mixture).astype(BF16)


def shards(
    queries,
    latent_cache,
    lengths,
    value_up,
    output_weight,
    residual,
    norm_gain,
    routed_experts,
    route_weights,
    gate_weight,
    up_weight,
    down_weight,
):
    swap = [(0, 1), (1, 0)]
    block = lax.axis_index("role") * TP + lax.axis_index("tp")
    place = jnp.stack([lax.axis_index("zh"), lax.axis_index("zl")]).astype(jnp.int32)

    residual_block = lax.dynamic_slice_in_dim(residual, block * ROWBLK, ROWBLK, 1)
    payload = jnp.concatenate(
        [output_weight, residual_block, jnp.zeros((COLS, 128 - ROWBLK), BF16)], axis=1
    )
    payloads = [payload] + [
        lax.ppermute(payload, "zh", [(i, (i + step) % ZH) for i in range(ZH)])
        for step in range(1, ZH)
    ]
    gain_rows = norm_gain.reshape(X, ZH, ZL, COLS).transpose(0, 2, 1, 3).reshape(X, 1, PLANE)
    own_in = jnp.concatenate([gate_weight[0], up_weight[0]], axis=1)
    own_in = (
        own_in.reshape(X, ZH, ZL, COLS, 256).transpose(0, 2, 1, 3, 4).reshape(X, PLANE, 256)
    )
    own_down = down_weight[0]
    peer_in = lax.ppermute(own_in, "role", swap)
    peer_down = lax.ppermute(own_down, "role", swap)
    routed_rows = lax.dynamic_slice_in_dim(routed_experts, block * ROWBLK, ROWBLK, 0).T
    route_rows = lax.dynamic_slice_in_dim(route_weights, block * ROWBLK, ROWBLK, 0).T
    pick, high, low = local_call(
        route_kernel,
        (shape((X * MOST, ROWBLK)), shape((Z * 32, 128)), shape((Z * 32, 128))),
        place,
        routed_rows,
        route_rows,
        scratch=(pltpu.VMEM((EXPERTS, ROWBLK), F32), pltpu.VMEM((EXPERTS, ROWBLK), F32)),
        smem=(0,),
    )

    heads = queries.shape[1]
    own_heads = heads // MEMBERS
    attended = local_call(
        attend_kernel, shape((heads, LAT)), lengths, queries, latent_cache.swapaxes(1, 2), smem=(0,)
    )
    attended = attended.reshape(MEMBERS, own_heads, LAT)
    regrouped = lax.all_to_all(attended, ("role", "tp"), 0, 0, tiled=True)
    values = local_call(
        value_kernel,
        shape((X * ZL, MEMBERS, own_heads * 128)),
        regrouped.reshape(MEMBERS * own_heads, LAT),
        value_up,
    )
    gathered = lax.all_to_all(values, ("x", "zl"), 0, 0, tiled=True)
    projected, residual_rows = local_call(
        project_kernel,
        (shape((X * ZL * MEMBERS, PART)), shape((ZL * TP, PART), F32)),
        place,
        gathered.reshape(X * ZL * MEMBERS, own_heads * 128),
        *payloads,
        scratch=(pltpu.VMEM((ZH,) + payload.shape, BF16),),
        smem=(0,),
    )
    head_parts = lax.all_to_all(
        projected.reshape(MEMBERS, ZL * TP, PART), ("role", "tp"), 0, 0, tiled=True
    )
    hidden = local_call(hidden_kernel, shape((Z, ZL * TP, PART)), head_parts, residual_rows)
    hidden = lax.all_to_all(hidden, ("zh", "zl"), 0, 0, tiled=True)
    outbound, own_hidden = local_call(
        dispatch_kernel,
        (shape((X * TP, MOST, PLANE)), shape((COLS, ROWBLK), F32)),
        place,
        hidden,
        pick,
        smem=(0,),
    )
    arrived = lax.all_to_all(outbound, ("x", "tp"), 0, 0, tiled=True)
    partial = local_call(
        expert_kernel,
        shape((X * TP, MOST, PLANE)),
        arrived,
        gain_rows,
        own_in,
        peer_in,
        own_down,
        peer_down,
    )
    hidden_parts = lax.all_to_all(partial, ("x", "tp"), 0, 0, tiled=True)
    columns = local_call(columns_kernel, shape((Z, 32, 128)), hidden_parts)
    returned = lax.all_to_all(columns, ("zh", "zl"), 0, 0, tiled=True)
    return local_call(
        combine_kernel,
        shape((COLS, ROWBLK)),
        returned.reshape(Z * 32, 128),
        high,
        low,
        own_hidden,
    )


def solution(mesh):
    grp = ("x", "zh", "zl")
    fine = Mesh(
        mesh.devices.reshape(ROLE, X, ZH, ZL, TP), ("role", "x", "zh", "zl", "tp")
    )
    return jax.shard_map(
        shards,
        mesh=fine,
        in_specs=(
            P(("role",) + grp + ("tp",), None, None),
            P(("role",) + grp + ("tp",), None, None),
            P(("role",) + grp + ("tp",)),
            P(("role", "tp"), None, None),
            P(grp, ("role", "tp")),
            P(grp, None),
            P(),
            P(),
            P(),
            P(grp, None, ("role", "tp")),
            P(grp, None, ("role", "tp")),
            P(grp, ("role", "tp"), None),
        ),
        out_specs=P(grp, ("role", "tp")),
        check_vma=False,
    )
```

```python
import jax
import jax.numpy as jnp
from jax import lax
from jax.experimental import pallas as pl
from jax.experimental.pallas import tpu as pltpu
from jax.sharding import Mesh
from jax.sharding import PartitionSpec as P

LAT = 512
SOFTMAX_SCALE = 192.0 ** (-0.5)
NORM_EPS = 1e-06

ROLE, X, Z, TP = 2, 4, 16, 4
MEMBERS = ROLE * TP
ROWBLK = 64
MOST = 16
EXPERTS = 64
COLS = 56
WIDTH = 3584
PLANE = Z * COLS
HALF = 64
PAYLOAD = 2432

F32 = jnp.float32
BF16 = jnp.bfloat16
VMEM_LIMIT = 48 * 1024 * 1024


def nt_dot(a, b):
    return lax.dot_general(a, b, (((1,), (1,)), ((), ())), preferred_element_type=F32)


def nn_dot(a, b):
    return lax.dot_general(a, b, (((1,), (0,)), ((), ())), preferred_element_type=F32)


def local_call(body, out_shape, *args, scratch=(), smem=()):
    specs = [
        pl.BlockSpec(memory_space=pltpu.SMEM if i in smem else pltpu.VMEM)
        for i in range(len(args))
    ]
    return pl.pallas_call(
        body,
        out_shape=out_shape,
        in_specs=specs,
        out_specs=jax.tree.map(lambda _: pl.BlockSpec(memory_space=pltpu.VMEM), out_shape),
        scratch_shapes=list(scratch),
        compiler_params=pltpu.CompilerParams(vmem_limit_bytes=VMEM_LIMIT),
    )(*args)


def shape(dims, dtype=BF16):
    return jax.ShapeDtypeStruct(dims, dtype)


def attend_kernel(length_ref, query_ref, cache_ref, out_ref):
    cache = cache_ref[0]
    scores = nn_dot(query_ref[0], cache) * SOFTMAX_SCALE
    visible = lax.broadcasted_iota(jnp.int32, scores.shape, 1) < length_ref[0]
    scores = jnp.where(visible, scores, -1e30)
    row_max = jnp.max(scores, axis=1, keepdims=True)
    weights = jnp.where(visible, jnp.exp(scores - row_max), 0.0)
    row_total = jnp.sum(weights, axis=1, keepdims=True)
    summed = nt_dot(weights.astype(BF16), cache[:LAT])
    out_ref[...] = (summed / row_total).astype(BF16)


def value_kernel(att_ref, value_ref, out_ref):
    heads = value_ref.shape[0]
    att = att_ref[...]
    rows = att.shape[0]
    row_head = lax.broadcasted_iota(jnp.int32, (rows, 128), 0) % heads
    for head in range(heads):
        product = nn_dot(att, value_ref[head])
        kept = jnp.where(row_head == head, product, 0.0)
        value = jnp.sum(kept.reshape(rows // heads, heads, 128), axis=1).astype(BF16)
        out_ref[:, :, head * 128 : (head + 1) * 128] = jnp.broadcast_to(
            value[None], (out_ref.shape[0],) + value.shape
        )


def packed(tile):
    gap = jnp.zeros((ROWBLK // 2, HALF - COLS), F32)
    return jnp.concatenate([tile[: ROWBLK // 2], gap, tile[ROWBLK // 2 :], gap], axis=1)


def project_kernel(place_ref, values_ref, payload_ref, out_ref, residual_ref):
    rows, depth = values_ref.shape
    place = lax.broadcasted_iota(jnp.int32, (rows, rows), 0)
    source = lax.broadcasted_iota(jnp.int32, (rows, rows), 1)
    lane = place % TP
    z = (place // TP) % Z
    role = place // (TP * Z)
    order = (source == z * MEMBERS + role * TP + lane).astype(F32).astype(BF16)
    values = nn_dot(order, values_ref[...]).astype(BF16)
    for x in range(X):
        product = nt_dot(values, payload_ref[x, :, :depth])
        for role in range(ROLE):
            tile = packed(product[role * ROWBLK : (role + 1) * ROWBLK])
            out_ref[role * X + x] = tile.astype(BF16)
    columns = payload_ref[place_ref[3], :, depth : depth + ROWBLK * MEMBERS]
    token = lax.broadcasted_iota(jnp.int32, (ROWBLK, ROWBLK * MEMBERS), 0)
    request = lax.broadcasted_iota(jnp.int32, (ROWBLK, ROWBLK * MEMBERS), 1)
    mine = request == token + (place_ref[2] * X + place_ref[0]) * ROWBLK
    residual_ref[...] = packed(nt_dot(mine.astype(F32).astype(BF16), columns))


def hidden_kernel(parts_ref, residual_ref, out_ref, own_ref):
    total = jnp.sum(parts_ref[...].astype(F32), axis=0)
    total = (residual_ref[...] + total).astype(BF16)
    own_ref[...] = total
    out_ref[...] = jnp.broadcast_to(total[None], out_ref.shape)


def route_kernel(
    place_ref, sent_ref, routed_ref, weight_ref, pick_ref, high_ref, low_ref, weights_ref, rank_ref
):
    dims = (EXPERTS, ROWBLK)
    expert_ids = lax.broadcasted_iota(jnp.int32, dims, 0)
    earlier = lax.broadcasted_iota(jnp.int32, (ROWBLK, ROWBLK), 0) < lax.broadcasted_iota(
        jnp.int32, (ROWBLK, ROWBLK), 1
    )
    before = jnp.where(earlier, 1.0, 0.0).astype(BF16)
    slots = lax.broadcasted_iota(jnp.int32, (MOST, ROWBLK), 0).astype(F32)

    def ranks(ids_ref):
        named = jnp.zeros(dims, F32)
        weights = jnp.zeros(dims, F32)
        for k in range(ids_ref.shape[0]):
            chosen = expert_ids == ids_ref[k : k + 1, :]
            named = named + jnp.where(chosen, 1.0, 0.0)
            weights = weights + jnp.where(chosen, weight_ref[k : k + 1, :], 0.0)
        rank = nn_dot(named.astype(BF16), before)
        return jnp.where(named > 0.5, rank, -1.0), weights

    rank_ref[...], _ = ranks(sent_ref)
    for x in range(X):
        row = rank_ref[pl.ds(x * Z + place_ref[1], 1), :]
        pick_ref[x * MOST : (x + 1) * MOST, :] = jnp.where(row == slots, 1.0, 0.0).astype(BF16)
    rank_ref[...], weights_ref[...] = ranks(routed_ref)
    for half in range(2):
        for z in range(Z):
            for pair in range(2):
                expert = (half * 2 + pair) * Z + z
                hit = rank_ref[expert : expert + 1, :] == slots
                table = jnp.where(hit, weights_ref[expert : expert + 1, :], 0.0)
                high = table.astype(BF16)
                low = (table - high.astype(F32)).astype(BF16)
                rows = pl.ds(z * 32 + pair * MOST, MOST)
                lanes = pl.ds(half * HALF, ROWBLK)
                high_ref[rows, lanes] = high
                low_ref[rows, lanes] = low


def dispatch_kernel(parts_ref, pick_ref, out_ref):
    parts = [parts_ref[z].astype(F32) for z in range(Z)]
    hidden = jnp.concatenate(
        [
            jnp.concatenate([part[:, start : start + COLS] for part in parts], axis=1)
            for start in (0, HALF)
        ],
        axis=0,
    ).astype(BF16)
    rows = nn_dot(pick_ref[...], hidden).astype(BF16)
    for x in range(X):
        piece = rows[x * MOST : (x + 1) * MOST]
        for lane in range(TP):
            out_ref[x * TP + lane] = piece


def expert_kernel(
    arrived_ref, gain_ref, own_in_ref, peer_in_ref, own_down_ref, peer_down_ref, out_ref
):
    rows = X * MOST
    values = []
    total = jnp.zeros((rows, 1), F32)
    for lane in range(TP):
        value = jnp.concatenate([arrived_ref[x * TP + lane] for x in range(X)], axis=0).astype(F32)
        total = total + jnp.sum(value * value, axis=1, keepdims=True)
        values.append(value)
    inverse = lax.rsqrt(total / WIDTH + NORM_EPS)
    own = jnp.zeros((rows, 256), F32)
    peer = jnp.zeros((rows, 256), F32)
    for i, value in enumerate(values):
        normed = (value * inverse * gain_ref[i]).astype(BF16)
        own = own + nn_dot(normed, own_in_ref[i])
        peer = peer + nn_dot(normed, peer_in_ref[i])

    def activate(both):
        gate, up = both[:, :128], both[:, 128:]
        return (gate / (1.0 + jnp.exp(-gate)) * up).astype(BF16)

    own_act, peer_act = activate(own), activate(peer)
    for x in range(X):
        lanes = pl.ds(x * PLANE, PLANE)
        product = nn_dot(own_act, own_down_ref[:, lanes]) + nn_dot(
            peer_act, peer_down_ref[:, lanes]
        )
        product = product.astype(BF16)
        for lane in range(TP):
            out_ref[x * TP + lane] = product[lane * MOST : (lane + 1) * MOST]


def columns_kernel(parts_ref, out_ref):
    summed = []
    for x in range(X):
        total = parts_ref[x * TP].astype(F32)
        for lane in range(1, TP):
            total = total + parts_ref[x * TP + lane].astype(F32)
        summed.append(total)
    low = jnp.concatenate(summed[:2], axis=0)
    high = jnp.concatenate(summed[2:], axis=0)
    gap = jnp.zeros((32, HALF - COLS), F32)
    for z in range(Z):
        cut = slice(z * COLS, (z + 1) * COLS)
        out_ref[z] = jnp.concatenate([low[:, cut], gap, high[:, cut], gap], axis=1).astype(BF16)


def combine_kernel(returned_ref, high_ref, low_ref, own_ref, out_ref):
    returned = returned_ref[...]
    dims = (((0,), (0,)), ((), ()))
    mixed = lax.dot_general(returned, high_ref[...], dims, preferred_element_type=F32)
    mixed = mixed + lax.dot_general(returned, low_ref[...], dims, preferred_element_type=F32)
    mixture = mixed[:COLS, :ROWBLK] + mixed[HALF : HALF + COLS, HALF : HALF + ROWBLK]
    column = lax.broadcasted_iota(jnp.int32, (COLS, 2 * HALF), 0)
    place = lax.broadcasted_iota(jnp.int32, (COLS, 2 * HALF), 1)
    own = own_ref[...]
    hidden = [
        nt_dot((place == column + start).astype(F32).astype(BF16), own) for start in (0, HALF)
    ]
    out_ref[...] = (jnp.concatenate(hidden, axis=1) + mixture).astype(BF16)


def shards(
    queries,
    latent_cache,
    lengths,
    value_up,
    output_weight,
    residual,
    norm_gain,
    routed_experts,
    route_weights,
    gate_weight,
    up_weight,
    down_weight,
):
    swap = [(0, 1), (1, 0)]
    role, x, z, lane = (lax.axis_index(name) for name in ("role", "x", "z", "tp"))
    place = jnp.stack([x, z, role, lane]).astype(jnp.int32)

    depth = output_weight.shape[1]
    payload = jnp.concatenate(
        [output_weight, residual, jnp.zeros((COLS, PAYLOAD - depth - residual.shape[1]), BF16)],
        axis=1,
    )
    payload = lax.all_gather(payload, "x", axis=0, tiled=True).reshape(X, COLS, PAYLOAD)
    gain_rows = norm_gain.reshape(TP, 1, PLANE)
    own_in = jnp.concatenate([gate_weight[0], up_weight[0]], axis=1).reshape(TP, PLANE, 256)
    own_down = down_weight[0]
    peer_in = lax.ppermute(own_in, "role", swap)
    peer_down = lax.ppermute(own_down, "role", swap)
    sent = lax.dynamic_slice_in_dim(routed_experts, (role * X + x) * ROWBLK, ROWBLK, 0).T
    block = (role * TP + lane) * ROWBLK
    routed = lax.dynamic_slice_in_dim(routed_experts, block, ROWBLK, 0).T
    weights = lax.dynamic_slice_in_dim(route_weights, block, ROWBLK, 0).T
    pick, high, low = local_call(
        route_kernel,
        (shape((X * MOST, ROWBLK)), shape((Z * 32, 128)), shape((Z * 32, 128))),
        place,
        sent,
        routed,
        weights,
        scratch=(pltpu.VMEM((EXPERTS, ROWBLK), F32), pltpu.VMEM((EXPERTS, ROWBLK), F32)),
        smem=(0,),
    )

    heads = queries.shape[1]
    own_heads = heads // MEMBERS
    attended = local_call(
        attend_kernel, shape((heads, LAT)), lengths, queries, latent_cache.swapaxes(1, 2), smem=(0,)
    )
    attended = attended.reshape(MEMBERS, own_heads, LAT)
    regrouped = lax.all_to_all(attended, ("role", "tp"), 0, 0, tiled=True)
    values = local_call(
        value_kernel,
        shape((Z, MEMBERS, own_heads * 128)),
        regrouped.reshape(MEMBERS * own_heads, LAT),
        value_up,
    )
    gathered = lax.all_to_all(values, "z", 0, 0, tiled=True)
    projected, residual_tile = local_call(
        project_kernel,
        (shape((MEMBERS, 32, 128)), shape((32, 128), F32)),
        place,
        gathered.reshape(Z * MEMBERS, own_heads * 128),
        payload,
        smem=(0,),
    )
    head_parts = lax.all_to_all(projected, ("role", "tp"), 0, 0, tiled=True)
    hidden, own = local_call(
        hidden_kernel, (shape((Z, 32, 128)), shape((32, 128))), head_parts, residual_tile
    )
    own = lax.ppermute(
        own, ("x", "tp"), [(a * TP + b, b * TP + a) for a in range(X) for b in range(TP)]
    )
    hidden = lax.all_to_all(hidden, "z", 0, 0, tiled=True)
    outbound = local_call(dispatch_kernel, shape((X * TP, MOST, PLANE)), hidden, pick)
    arrived = lax.all_to_all(outbound, ("x", "tp"), 0, 0, tiled=True)
    partial = local_call(
        expert_kernel,
        shape((X * TP, MOST, PLANE)),
        arrived,
        gain_rows,
        own_in,
        peer_in,
        own_down,
        peer_down,
    )
    hidden_parts = lax.all_to_all(partial, ("x", "tp"), 0, 0, tiled=True)
    columns = local_call(columns_kernel, shape((Z, 32, 128)), hidden_parts)
    returned = lax.all_to_all(columns, "z", 0, 0, tiled=True)
    return local_call(
        combine_kernel,
        shape((COLS, ROWBLK)),
        returned.reshape(Z * 32, 128),
        high,
        low,
        own,
    )


def solution(mesh):
    grp = ("x", "z")
    fine = Mesh(mesh.devices.reshape(ROLE, X, Z, TP), ("role", "x", "z", "tp"))
    return jax.shard_map(
        shards,
        mesh=fine,
        in_specs=(
            P(("role",) + grp + ("tp",), None, None),
            P(("role",) + grp + ("tp",), None, None),
            P(("role",) + grp + ("tp",)),
            P(("role", "tp"), None, None),
            P(grp, ("role", "tp")),
            P(grp, None),
            P(),
            P(),
            P(),
            P(grp, None, ("role", "tp")),
            P(grp, None, ("role", "tp")),
            P(grp, ("role", "tp"), None),
        ),
        out_specs=P(grp, ("role", "tp")),
        check_vma=False,
    )
```

```python
import jax
import jax.numpy as jnp
from jax import lax
from jax.experimental import pallas as pl
from jax.experimental.pallas import tpu as pltpu
from jax.sharding import Mesh
from jax.sharding import PartitionSpec as P

LAT = 512
SOFTMAX_SCALE = 192.0 ** (-0.5)
NORM_EPS = 1e-06

ROLE, X, Z, TP = 2, 4, 16, 4
MEMBERS = ROLE * TP
ROWBLK = 64
MOST = 16
EXPERTS = 64
COLS = 56
WIDTH = 3584
PLANE = Z * COLS
HALF = 64

Z_FIRST, X_FIRST, TP_FIRST = 8, 2, 2
Z_ORDER = [(i + Z_FIRST) % Z for i in range(Z)]
HEAD_ORDER = [
    (1 - role) * TP + (lane + TP_FIRST) % TP for role in range(ROLE) for lane in range(TP)
]
PLANE_ORDER = [
    (x + X_FIRST) % X * TP + (lane + TP_FIRST) % TP for x in range(X) for lane in range(TP)
]
Z_AT = [Z_ORDER.index(z) for z in range(Z)]
HEAD_AT = [HEAD_ORDER.index(i) for i in range(MEMBERS)]
PLANE_AT = [[PLANE_ORDER.index(x * TP + lane) for lane in range(TP)] for x in range(X)]

F32 = jnp.float32
BF16 = jnp.bfloat16
VMEM_LIMIT = 48 * 1024 * 1024
ALL_VMEM = 60 * 1024 * 1024


def nt_dot(a, b):
    return lax.dot_general(a, b, (((1,), (1,)), ((), ())), preferred_element_type=F32)


def nn_dot(a, b):
    return lax.dot_general(a, b, (((1,), (0,)), ((), ())), preferred_element_type=F32)


def local_call(
    body, out_shape, *args, scratch=(), smem=(), hbm=(), out_hbm=(), vmem=VMEM_LIMIT
):
    def space(i, smem, hbm):
        return pltpu.SMEM if i in smem else pltpu.HBM if i in hbm else pltpu.VMEM

    many = isinstance(out_shape, tuple)
    outs = [
        pl.BlockSpec(memory_space=space(i, (), out_hbm))
        for i in range(len(out_shape) if many else 1)
    ]
    return pl.pallas_call(
        body,
        out_shape=out_shape,
        in_specs=[pl.BlockSpec(memory_space=space(i, smem, hbm)) for i in range(len(args))],
        out_specs=tuple(outs) if many else outs[0],
        scratch_shapes=list(scratch),
        compiler_params=pltpu.CompilerParams(vmem_limit_bytes=vmem),
    )(*args)


def exchange(chunks, axes, order):
    return lax.all_to_all(chunks, axes, 0, 0, tiled=True, axis_index_groups=[order])


def shape(dims, dtype=BF16):
    return jax.ShapeDtypeStruct(dims, dtype)


def attend_kernel(
    length_ref,
    query_hbm,
    cache_hbm,
    weight_hbm,
    residual_hbm,
    out_ref,
    payload_hbm,
    query_ref,
    cache_ref,
    sems,
):
    depth = weight_hbm.shape[1]
    span = residual_hbm.shape[1] // ROLE
    start = pl.multiple_of(lax.axis_index("role") * span, span)
    copies = [
        pltpu.make_async_copy(cache_hbm.at[0], cache_ref, sems.at[0]),
        pltpu.make_async_copy(query_hbm.at[0], query_ref, sems.at[1]),
        pltpu.make_async_copy(weight_hbm, payload_hbm.at[:, pl.ds(0, depth)], sems.at[2]),
        pltpu.make_async_copy(
            residual_hbm.at[:, pl.ds(start, span)], payload_hbm.at[:, pl.ds(depth, span)], sems.at[3]
        ),
    ]
    for copy in copies:
        copy.start()
    copies[0].wait()
    copies[1].wait()
    scores = nn_dot(query_ref[...], cache_ref[...]) * SOFTMAX_SCALE
    visible = lax.broadcasted_iota(jnp.int32, scores.shape, 1) < length_ref[0]
    scores = jnp.where(visible, scores, -1e30)
    row_max = jnp.max(scores, axis=1, keepdims=True)
    weights = jnp.where(visible, jnp.exp(scores - row_max), 0.0)
    row_total = jnp.sum(weights, axis=1, keepdims=True)
    summed = nt_dot(weights.astype(BF16), cache_ref[:LAT])
    attended = summed / row_total
    heads = attended.shape[0] // MEMBERS
    attended = [attended[i * heads : (i + 1) * heads] for i in HEAD_ORDER]
    out_ref[...] = jnp.concatenate(attended, axis=0).astype(BF16)
    for copy in copies[2:]:
        copy.wait()


def value_kernel(att_ref, value_ref, out_ref):
    heads = value_ref.shape[0]
    att = att_ref[...]
    rows = att.shape[0]
    row_head = lax.broadcasted_iota(jnp.int32, (rows, 256), 0) % heads
    lane_head = lax.broadcasted_iota(jnp.int32, (rows, 256), 1) // 128
    for head in range(0, heads, 2):
        pair = jnp.concatenate([value_ref[head], value_ref[head + 1]], axis=1)
        kept = jnp.where(row_head == head + lane_head, nn_dot(att, pair), 0.0)
        value = jnp.sum(kept.reshape(rows // heads, heads, 256), axis=1)
        value = jnp.concatenate([value[i : i + 1] for i in HEAD_AT], axis=0).astype(BF16)
        out_ref[:, :, head * 128 : (head + 2) * 128] = jnp.broadcast_to(
            value[None], (out_ref.shape[0],) + value.shape
        )


def packed(tile):
    gap = jnp.zeros((ROWBLK // 2, HALF - COLS), F32)
    return jnp.concatenate([tile[: ROWBLK // 2], gap, tile[ROWBLK // 2 :], gap], axis=1)


def by_source(refs):
    for step, ref in zip((0, 2, 3, 1), refs):
        yield lax.rem(lax.axis_index("x") + step, X), ref


def project_kernel(values_ref, *refs):
    weights, out_ref = refs[:X], refs[X]
    depth = values_ref.shape[1]
    values = values_ref[...]
    for x, weight in by_source(weights):
        product = nt_dot(values, weight[:, :depth]).reshape(Z, MEMBERS, COLS)
        lane = lax.rem(x + TP - TP_FIRST, TP)
        for role in range(ROLE):
            tile = jnp.concatenate(
                [product[Z_AT[z], role * TP : (role + 1) * TP] for z in range(Z)], axis=0
            )
            out_ref[(1 - role) * TP + lane] = packed(tile).astype(BF16)


def residual_kernel(own_ref, *refs):
    payloads, out_ref = refs[: X - 1], refs[X - 1]
    span = ROWBLK * X
    token = lax.broadcasted_iota(jnp.int32, (ROWBLK, span), 0)
    request = lax.broadcasted_iota(jnp.int32, (ROWBLK, span), 1)
    mine = request == token + lax.axis_index("x") * ROWBLK
    start = pl.multiple_of(lax.axis_index("role") * span, span)
    columns = [own_ref[:, pl.ds(start, span)]]
    columns += [payload[:, payload.shape[1] - span :] for payload in payloads]
    total = jnp.zeros((ROWBLK, COLS), F32)
    for x, column in by_source(columns):
        wanted = mine & (x == lax.axis_index("tp"))
        total = total + nt_dot(jnp.where(wanted, 1.0, 0.0).astype(BF16), column)
    out_ref[...] = packed(total)


def hidden_kernel(parts_ref, residual_ref, out_ref, own_ref):
    total = jnp.sum(parts_ref[...].astype(F32), axis=0)
    total = (residual_ref[...] + total).astype(BF16)
    own_ref[...] = total
    out_ref[...] = jnp.broadcast_to(total[None], out_ref.shape)


def route_kernel(
    sent_ref, routed_ref, weight_ref, pick_ref, high_ref, low_ref, weights_ref, rank_ref
):
    dims = (EXPERTS, ROWBLK)
    expert_ids = lax.broadcasted_iota(jnp.int32, dims, 0)
    earlier = lax.broadcasted_iota(jnp.int32, (ROWBLK, ROWBLK), 0) < lax.broadcasted_iota(
        jnp.int32, (ROWBLK, ROWBLK), 1
    )
    before = jnp.where(earlier, 1.0, 0.0).astype(BF16)
    slots = lax.broadcasted_iota(jnp.int32, (MOST, ROWBLK), 0).astype(F32)

    def ranks(ids_ref):
        named = jnp.zeros(dims, F32)
        weights = jnp.zeros(dims, F32)
        for k in range(ids_ref.shape[0]):
            chosen = expert_ids == ids_ref[k : k + 1, :]
            named = named + jnp.where(chosen, 1.0, 0.0)
            weights = weights + jnp.where(chosen, weight_ref[k : k + 1, :], 0.0)
        rank = nn_dot(named.astype(BF16), before)
        return jnp.where(named > 0.5, rank, -1.0), weights

    rank_ref[...], _ = ranks(sent_ref)
    for x in range(X):
        row = rank_ref[pl.ds(x * Z + lax.axis_index("z"), 1), :]
        pick_ref[x * MOST : (x + 1) * MOST, :] = jnp.where(row == slots, 1.0, 0.0).astype(BF16)
    rank_ref[...], weights_ref[...] = ranks(routed_ref)
    for half in range(2):
        for z in range(Z):
            for pair in range(2):
                expert = (half * 2 + pair) * Z + z
                hit = rank_ref[expert : expert + 1, :] == slots
                table = jnp.where(hit, weights_ref[expert : expert + 1, :], 0.0)
                high = table.astype(BF16)
                low = (table - high.astype(F32)).astype(BF16)
                rows = pl.ds(Z_AT[z] * 32 + pair * MOST, MOST)
                lanes = pl.ds(half * HALF, ROWBLK)
                high_ref[rows, lanes] = high
                low_ref[rows, lanes] = low


def dispatch_kernel(parts_ref, pick_ref, own_ref, out_ref):
    parts = [parts_ref[Z_AT[z]].astype(F32) for z in range(Z)]
    hidden = jnp.concatenate(
        [
            jnp.concatenate([part[:, start : start + COLS] for part in parts], axis=1)
            for start in (0, HALF)
        ],
        axis=0,
    ).astype(BF16)
    rows = nn_dot(pick_ref[...], hidden).astype(BF16)
    own = own_ref[...]
    for x in range(X):
        piece = jnp.concatenate([rows[x * MOST : (x + 1) * MOST], own[:MOST], own[MOST:]], axis=1)
        for lane in range(TP):
            out_ref[PLANE_AT[x][lane]] = piece


def expert_kernel(arrived_ref, gain_ref, *refs):
    own_refs, peer_refs, (out_ref, tile_ref) = refs[:3], refs[3:6], refs[6:]
    x = lax.rem(lax.axis_index("tp") + X - X_FIRST, X)
    lane = lax.rem(lax.axis_index("x") + TP - TP_FIRST, TP)
    tile = arrived_ref[x * TP + lane]
    tile_ref[:MOST] = tile[:, PLANE : PLANE + 128]
    tile_ref[MOST:] = tile[:, PLANE + 128 :]
    rows = X * MOST
    total = jnp.zeros((rows, 1), F32)
    own = jnp.zeros((rows, 256), F32)
    peer = jnp.zeros((rows, 256), F32)
    for lane in range(TP):
        value = jnp.concatenate(
            [arrived_ref[PLANE_AT[x][lane], :, :PLANE] for x in range(X)], axis=0
        ).astype(F32)
        depth = pl.ds(lane * PLANE, PLANE)
        total = total + jnp.sum(value * value, axis=1, keepdims=True)
        scaled = (value * gain_ref[lane]).astype(BF16)
        own, peer = [
            so_far + nn_dot(scaled, jnp.concatenate([refs[0][depth], refs[1][depth]], axis=1))
            for so_far, refs in ((own, own_refs), (peer, peer_refs))
        ]
    inverse = lax.rsqrt(total / WIDTH + NORM_EPS)

    def activate(both):
        both = both * inverse
        gate, up = both[:, :128], both[:, 128:]
        return (gate / (1.0 + jnp.exp(-gate)) * up).astype(BF16)

    activated = jnp.concatenate([activate(own), activate(peer)], axis=1)
    for x in range(X):
        lanes = slice(x * PLANE, (x + 1) * PLANE)
        down = jnp.concatenate([own_refs[2][:, lanes], peer_refs[2][:, lanes]], axis=0)
        product = nn_dot(activated, down).astype(BF16)
        for lane in range(TP):
            out_ref[PLANE_AT[x][lane]] = product[lane * MOST : (lane + 1) * MOST]


def columns_kernel(parts_ref, out_ref):
    summed = []
    for x in range(X):
        total = parts_ref[PLANE_AT[x][0]].astype(F32)
        for lane in range(1, TP):
            total = total + parts_ref[PLANE_AT[x][lane]].astype(F32)
        summed.append(total)
    low = jnp.concatenate(summed[:2], axis=0)
    high = jnp.concatenate(summed[2:], axis=0)
    gap = jnp.zeros((32, HALF - COLS), F32)
    for z in range(Z):
        cut = slice(z * COLS, (z + 1) * COLS)
        out_ref[Z_AT[z]] = jnp.concatenate([low[:, cut], gap, high[:, cut], gap], axis=1).astype(BF16)


def combine_kernel(returned_ref, high_ref, low_ref, own_ref, out_ref):
    returned = returned_ref[...]
    dims = (((0,), (0,)), ((), ()))
    mixed = lax.dot_general(returned, high_ref[...], dims, preferred_element_type=F32)
    mixed = mixed + lax.dot_general(returned, low_ref[...], dims, preferred_element_type=F32)
    mixture = mixed[:COLS, :ROWBLK] + mixed[HALF : HALF + COLS, HALF : HALF + ROWBLK]
    column = lax.broadcasted_iota(jnp.int32, (COLS, 2 * HALF), 0)
    place = lax.broadcasted_iota(jnp.int32, (COLS, 2 * HALF), 1)
    own = own_ref[...]
    hidden = [
        nt_dot((place == column + start).astype(F32).astype(BF16), own) for start in (0, HALF)
    ]
    out_ref[...] = (jnp.concatenate(hidden, axis=1) + mixture).astype(BF16)


def shards(
    queries,
    latent_cache,
    lengths,
    value_up,
    output_weight,
    residual,
    norm_gain,
    routed_experts,
    route_weights,
    gate_weight,
    up_weight,
    down_weight,
):
    swap = [(0, 1), (1, 0)]
    role, x, lane = (lax.axis_index(name) for name in ("role", "x", "tp"))

    sent = lax.dynamic_slice_in_dim(routed_experts, (role * X + x) * ROWBLK, ROWBLK, 0).T
    block = (role * TP + lane) * ROWBLK
    routed = lax.dynamic_slice_in_dim(routed_experts, block, ROWBLK, 0).T
    weights = lax.dynamic_slice_in_dim(route_weights, block, ROWBLK, 0).T
    pick, high, low = local_call(
        route_kernel,
        (shape((X * MOST, ROWBLK)), shape((Z * 32, 128)), shape((Z * 32, 128))),
        sent,
        routed,
        weights,
        scratch=(pltpu.VMEM((EXPERTS, ROWBLK), F32), pltpu.VMEM((EXPERTS, ROWBLK), F32)),
    )

    heads = queries.shape[1]
    own_heads = heads // MEMBERS
    width = output_weight.shape[1] + residual.shape[1] // ROLE
    attended, payload = local_call(
        attend_kernel,
        (shape((heads, LAT)), shape((COLS, width))),
        lengths,
        queries,
        latent_cache.swapaxes(1, 2),
        output_weight,
        residual,
        scratch=(
            pltpu.VMEM(queries.shape[1:], BF16),
            pltpu.VMEM(latent_cache.shape[:0:-1], BF16),
            pltpu.SemaphoreType.DMA((4,)),
        ),
        smem=(0,),
        hbm=(1, 2, 3, 4),
        vmem=ALL_VMEM,
    )
    attended = attended.reshape(MEMBERS, own_heads, LAT)
    across = lax.ppermute(payload, "x", [(i, (i + 2) % X) for i in range(X)])
    regrouped = exchange(attended, ("role", "tp"), HEAD_ORDER)
    regrouped, across = lax.optimization_barrier((regrouped, across))
    values = local_call(
        value_kernel,
        shape((Z, MEMBERS, own_heads * 128)),
        regrouped.reshape(MEMBERS * own_heads, LAT),
        value_up,
    )
    payloads = [across] + [
        lax.ppermute(payload, "x", [(i, (i + step) % X) for i in range(X)]) for step in (1, 3)
    ]
    gathered = exchange(values, "z", Z_ORDER)
    projected = local_call(
        project_kernel,
        shape((MEMBERS, 32, 128)),
        gathered.reshape(Z * MEMBERS, own_heads * 128),
        output_weight,
        *payloads,
    )
    residual_tile = local_call(
        residual_kernel, shape((32, 128), F32), residual, *payloads
    )
    head_parts = exchange(projected, ("role", "tp"), HEAD_ORDER)
    hidden, own = local_call(
        hidden_kernel, (shape((Z, 32, 128)), shape((32, 128))), head_parts, residual_tile
    )

    gain_rows = norm_gain.reshape(TP, 1, PLANE)
    own_expert = (gate_weight[0], up_weight[0], down_weight[0])
    peer_expert = [lax.ppermute(weight, "role", swap) for weight in own_expert]
    hidden = exchange(hidden, "z", Z_ORDER)
    outbound = local_call(
        dispatch_kernel, shape((X * TP, MOST, PLANE + 256)), hidden, pick, own
    )
    arrived = exchange(outbound, ("x", "tp"), PLANE_ORDER)
    partial, own = local_call(
        expert_kernel,
        (shape((X * TP, MOST, PLANE)), shape((32, 128))),
        arrived,
        gain_rows,
        *own_expert,
        *peer_expert,
    )
    hidden_parts = exchange(partial, ("x", "tp"), PLANE_ORDER)
    columns = local_call(columns_kernel, shape((Z, 32, 128)), hidden_parts)
    returned = exchange(columns, "z", Z_ORDER)
    return local_call(
        combine_kernel,
        shape((COLS, ROWBLK)),
        returned.reshape(Z * 32, 128),
        high,
        low,
        own,
    )


def solution(mesh):
    grp = ("x", "z")
    fine = Mesh(mesh.devices.reshape(ROLE, X, Z, TP), ("role", "x", "z", "tp"))
    return jax.shard_map(
        shards,
        mesh=fine,
        in_specs=(
            P(("role",) + grp + ("tp",), None, None),
            P(("role",) + grp + ("tp",), None, None),
            P(("role",) + grp + ("tp",)),
            P(("role", "tp"), None, None),
            P(grp, ("role", "tp")),
            P(grp, None),
            P(),
            P(),
            P(),
            P(grp, None, ("role", "tp")),
            P(grp, None, ("role", "tp")),
            P(grp, ("role", "tp"), None),
        ),
        out_specs=P(grp, ("role", "tp")),
        check_vma=False,
    )
```

```python
import jax
import jax.numpy as jnp
from jax import lax
from jax.experimental import pallas as pl
from jax.experimental.pallas import tpu as pltpu
from jax.sharding import Mesh
from jax.sharding import PartitionSpec as P

LAT = 512
SOFTMAX_SCALE = 192.0 ** (-0.5)
NORM_EPS = 1e-06

ROLE, X, Z, TP = 2, 4, 16, 4
MEMBERS = ROLE * TP
ROWBLK = 64
MOST = 16
EXPERTS = 64
COLS = 56
WIDTH = 3584
PLANE = Z * COLS
HALF = 64

VALUE_FIRST, HIDDEN_FIRST, RETURN_FIRST = 8, 4, 8
X_FIRST, TP_FIRST = 2, 2


def z_order(first):
    return [(i + first) % Z for i in range(Z)]


def z_places(first):
    return [(z - first) % Z for z in range(Z)]


HEAD_ORDER = [
    (1 - role) * TP + (lane + TP_FIRST) % TP for role in range(ROLE) for lane in range(TP)
]
PLANE_ORDER = [
    (x + X_FIRST) % X * TP + (lane + TP_FIRST) % TP for x in range(X) for lane in range(TP)
]
HEAD_AT = [HEAD_ORDER.index(i) for i in range(MEMBERS)]
PLANE_AT = [[PLANE_ORDER.index(x * TP + lane) for lane in range(TP)] for x in range(X)]

F32 = jnp.float32
BF16 = jnp.bfloat16
VMEM_LIMIT = 16 * 1024 * 1024
ALL_VMEM = 60 * 1024 * 1024


def nt_dot(a, b):
    return lax.dot_general(a, b, (((1,), (1,)), ((), ())), preferred_element_type=F32)


def nn_dot(a, b):
    return lax.dot_general(a, b, (((1,), (0,)), ((), ())), preferred_element_type=F32)


def local_call(
    body, out_shape, *args, scratch=(), smem=(), hbm=(), out_hbm=(), vmem=VMEM_LIMIT
):
    def space(i, smem, hbm):
        return pltpu.SMEM if i in smem else pltpu.HBM if i in hbm else pltpu.VMEM

    many = isinstance(out_shape, tuple)
    outs = [
        pl.BlockSpec(memory_space=space(i, (), out_hbm))
        for i in range(len(out_shape) if many else 1)
    ]
    return pl.pallas_call(
        body,
        out_shape=out_shape,
        in_specs=[pl.BlockSpec(memory_space=space(i, smem, hbm)) for i in range(len(args))],
        out_specs=tuple(outs) if many else outs[0],
        scratch_shapes=list(scratch),
        compiler_params=pltpu.CompilerParams(vmem_limit_bytes=vmem),
    )(*args)


def exchange(chunks, axes, order):
    return lax.all_to_all(chunks, axes, 0, 0, tiled=True, axis_index_groups=[order])


def shape(dims, dtype=BF16):
    return jax.ShapeDtypeStruct(dims, dtype)


def attend_kernel(
    length_ref,
    query_hbm,
    cache_hbm,
    weight_hbm,
    residual_hbm,
    out_ref,
    payload_hbm,
    query_ref,
    cache_ref,
    sems,
):
    depth = weight_hbm.shape[1]
    span = residual_hbm.shape[1] // ROLE
    start = pl.multiple_of(lax.axis_index("role") * span, span)
    copies = [
        pltpu.make_async_copy(cache_hbm.at[0], cache_ref, sems.at[0]),
        pltpu.make_async_copy(query_hbm.at[0], query_ref, sems.at[1]),
        pltpu.make_async_copy(weight_hbm, payload_hbm.at[:, pl.ds(0, depth)], sems.at[2]),
        pltpu.make_async_copy(
            residual_hbm.at[:, pl.ds(start, span)], payload_hbm.at[:, pl.ds(depth, span)], sems.at[3]
        ),
    ]
    for copy in copies:
        copy.start()
    copies[0].wait()
    copies[1].wait()
    scores = nn_dot(query_ref[...], cache_ref[...]) * SOFTMAX_SCALE
    visible = lax.broadcasted_iota(jnp.int32, scores.shape, 1) < length_ref[0]
    scores = jnp.where(visible, scores, -1e30)
    row_max = jnp.max(scores, axis=1, keepdims=True)
    weights = jnp.where(visible, jnp.exp(scores - row_max), 0.0)
    row_total = jnp.sum(weights, axis=1, keepdims=True)
    summed = nt_dot(weights.astype(BF16), cache_ref[:LAT])
    attended = summed / row_total
    heads = attended.shape[0] // MEMBERS
    attended = [attended[i * heads : (i + 1) * heads] for i in HEAD_ORDER]
    out_ref[...] = jnp.concatenate(attended, axis=0).astype(BF16)
    for copy in copies[2:]:
        copy.wait()


def value_kernel(att_ref, value_ref, out_ref):
    heads = value_ref.shape[0]
    att = att_ref[...]
    rows = att.shape[0]
    row_head = lax.broadcasted_iota(jnp.int32, (rows, 256), 0) % heads
    lane_head = lax.broadcasted_iota(jnp.int32, (rows, 256), 1) // 128
    for head in range(0, heads, 2):
        pair = jnp.concatenate([value_ref[head], value_ref[head + 1]], axis=1)
        kept = jnp.where(row_head == head + lane_head, nn_dot(att, pair), 0.0)
        value = jnp.sum(kept.reshape(rows // heads, heads, 256), axis=1)
        value = jnp.concatenate([value[i : i + 1] for i in HEAD_AT], axis=0).astype(BF16)
        out_ref[:, :, head * 128 : (head + 2) * 128] = jnp.broadcast_to(
            value[None], (out_ref.shape[0],) + value.shape
        )


def packed(tile):
    gap = jnp.zeros((ROWBLK // 2, HALF - COLS), F32)
    return jnp.concatenate([tile[: ROWBLK // 2], gap, tile[ROWBLK // 2 :], gap], axis=1)


def by_source(refs):
    for step, ref in zip((0, 2, 3, 1), refs):
        yield lax.rem(lax.axis_index("x") + step, X), ref


def project_kernel(values_ref, *refs):
    weights, out_ref = refs[:X], refs[X]
    depth = values_ref.shape[1]
    values = values_ref[...]
    for x, weight in by_source(weights):
        product = nt_dot(values, weight[:, :depth]).reshape(Z, MEMBERS, COLS)
        lane = lax.rem(x + TP - TP_FIRST, TP)
        for role in range(ROLE):
            tile = jnp.concatenate(
                [product[at, role * TP : (role + 1) * TP] for at in z_places(VALUE_FIRST)], axis=0
            )
            out_ref[(1 - role) * TP + lane] = packed(tile).astype(BF16)


def residual_kernel(own_ref, *refs):
    payloads, out_ref = refs[: X - 1], refs[X - 1]
    span = ROWBLK * X
    token = lax.broadcasted_iota(jnp.int32, (ROWBLK, span), 0)
    request = lax.broadcasted_iota(jnp.int32, (ROWBLK, span), 1)
    mine = request == token + lax.axis_index("x") * ROWBLK
    start = pl.multiple_of(lax.axis_index("role") * span, span)
    columns = [own_ref[:, pl.ds(start, span)]]
    columns += [payload[:, payload.shape[1] - span :] for payload in payloads]
    total = jnp.zeros((ROWBLK, COLS), F32)
    for x, column in by_source(columns):
        wanted = mine & (x == lax.axis_index("tp"))
        total = total + nt_dot(jnp.where(wanted, 1.0, 0.0).astype(BF16), column)
    out_ref[...] = packed(total)


def hidden_kernel(parts_ref, residual_ref, out_ref, own_ref):
    total = jnp.sum(parts_ref[...].astype(F32), axis=0)
    total = (residual_ref[...] + total).astype(BF16)
    own_ref[...] = total
    out_ref[...] = jnp.broadcast_to(total[None], out_ref.shape)


def route_kernel(
    sent_ref, routed_ref, weight_ref, pick_ref, high_ref, low_ref, weights_ref, rank_ref
):
    dims = (EXPERTS, ROWBLK)
    expert_ids = lax.broadcasted_iota(jnp.int32, dims, 0)
    earlier = lax.broadcasted_iota(jnp.int32, (ROWBLK, ROWBLK), 0) < lax.broadcasted_iota(
        jnp.int32, (ROWBLK, ROWBLK), 1
    )
    before = jnp.where(earlier, 1.0, 0.0).astype(BF16)
    slots = lax.broadcasted_iota(jnp.int32, (MOST, ROWBLK), 0).astype(F32)

    def ranks(ids_ref):
        named = jnp.zeros(dims, F32)
        weights = jnp.zeros(dims, F32)
        for k in range(ids_ref.shape[0]):
            chosen = expert_ids == ids_ref[k : k + 1, :]
            named = named + jnp.where(chosen, 1.0, 0.0)
            weights = weights + jnp.where(chosen, weight_ref[k : k + 1, :], 0.0)
        rank = nn_dot(named.astype(BF16), before)
        return jnp.where(named > 0.5, rank, -1.0), weights

    rank_ref[...], _ = ranks(sent_ref)
    for x in range(X):
        row = rank_ref[pl.ds(x * Z + lax.axis_index("z"), 1), :]
        pick_ref[x * MOST : (x + 1) * MOST, :] = jnp.where(row == slots, 1.0, 0.0).astype(BF16)
    rank_ref[...], weights_ref[...] = ranks(routed_ref)
    for half in range(2):
        for z in range(Z):
            for pair in range(2):
                expert = (half * 2 + pair) * Z + z
                hit = rank_ref[expert : expert + 1, :] == slots
                table = jnp.where(hit, weights_ref[expert : expert + 1, :], 0.0)
                high = table.astype(BF16)
                low = (table - high.astype(F32)).astype(BF16)
                rows = pl.ds(z_places(RETURN_FIRST)[z] * 32 + pair * MOST, MOST)
                lanes = pl.ds(half * HALF, ROWBLK)
                high_ref[rows, lanes] = high
                low_ref[rows, lanes] = low


def dispatch_kernel(parts_ref, pick_ref, out_ref):
    parts = [parts_ref[at].astype(F32) for at in z_places(HIDDEN_FIRST)]
    hidden = jnp.concatenate(
        [
            jnp.concatenate([part[:, start : start + COLS] for part in parts], axis=1)
            for start in (0, HALF)
        ],
        axis=0,
    ).astype(BF16)
    rows = nn_dot(pick_ref[...], hidden).astype(BF16)
    for x in range(X):
        piece = rows[x * MOST : (x + 1) * MOST]
        for lane in range(TP):
            out_ref[PLANE_AT[x][lane]] = piece


def expert_kernel(arrived_ref, gain_ref, *refs):
    own_refs, peer_refs, out_ref = refs[:3], refs[3:6], refs[6]
    rows = X * MOST
    total = jnp.zeros((rows, 1), F32)
    scaled = []
    for lane in range(TP):
        value = jnp.concatenate(
            [arrived_ref[PLANE_AT[x][lane]] for x in range(X)], axis=0
        ).astype(F32)
        total = total + jnp.sum(value * value, axis=1, keepdims=True)
        scaled.append((value * gain_ref[lane]).astype(BF16))

    def hidden_sums(refs):
        sums = jnp.zeros((rows, 256), F32)
        for lane in range(TP):
            depth = pl.ds(lane * PLANE, PLANE)
            both = jnp.concatenate([refs[0][depth], refs[1][depth]], axis=1)
            sums = sums + nn_dot(scaled[lane], both)
        return sums

    own, peer = hidden_sums(own_refs), hidden_sums(peer_refs)
    inverse = lax.rsqrt(total / WIDTH + NORM_EPS)

    def activate(both):
        both = both * inverse
        gate, up = both[:, :128], both[:, 128:]
        return (gate / (1.0 + jnp.exp(-gate)) * up).astype(BF16)

    activated = jnp.concatenate([activate(own), activate(peer)], axis=1)
    for x in range(X):
        lanes = slice(x * PLANE, (x + 1) * PLANE)
        down = jnp.concatenate([own_refs[2][:, lanes], peer_refs[2][:, lanes]], axis=0)
        product = nn_dot(activated, down).astype(BF16)
        for lane in range(TP):
            out_ref[PLANE_AT[x][lane]] = product[lane * MOST : (lane + 1) * MOST]


def columns_kernel(parts_ref, out_ref):
    summed = []
    for x in range(X):
        total = parts_ref[PLANE_AT[x][0]].astype(F32)
        for lane in range(1, TP):
            total = total + parts_ref[PLANE_AT[x][lane]].astype(F32)
        summed.append(total)
    low = jnp.concatenate(summed[:2], axis=0)
    high = jnp.concatenate(summed[2:], axis=0)
    gap = jnp.zeros((32, HALF - COLS), F32)
    for z in range(Z):
        cut = slice(z * COLS, (z + 1) * COLS)
        out_ref[z_places(RETURN_FIRST)[z]] = jnp.concatenate([low[:, cut], gap, high[:, cut], gap], axis=1).astype(BF16)


def combine_kernel(returned_ref, high_ref, low_ref, own_ref, out_ref):
    returned = returned_ref[...]
    dims = (((0,), (0,)), ((), ()))
    mixed = lax.dot_general(returned, high_ref[...], dims, preferred_element_type=F32)
    mixed = mixed + lax.dot_general(returned, low_ref[...], dims, preferred_element_type=F32)
    mixture = mixed[:COLS, :ROWBLK] + mixed[HALF : HALF + COLS, HALF : HALF + ROWBLK]
    column = lax.broadcasted_iota(jnp.int32, (COLS, 2 * HALF), 0)
    place = lax.broadcasted_iota(jnp.int32, (COLS, 2 * HALF), 1)
    own = own_ref[...]
    hidden = [
        nt_dot((place == column + start).astype(F32).astype(BF16), own) for start in (0, HALF)
    ]
    out_ref[...] = (jnp.concatenate(hidden, axis=1) + mixture).astype(BF16)


def preload_kernel(*refs):
    count = (len(refs) - 1) // 2
    sems = refs[-1]
    copies = [
        pltpu.make_async_copy(refs[i], refs[count + i], sems.at[i]) for i in range(count)
    ]
    for copy in copies:
        copy.start()
    for copy in copies:
        copy.wait()


def preload(*arrays):
    return local_call(
        preload_kernel,
        tuple(shape(array.shape, array.dtype) for array in arrays),
        *arrays,
        scratch=(pltpu.SemaphoreType.DMA((len(arrays),)),),
        hbm=range(len(arrays)),
    )


def shards(
    queries,
    latent_cache,
    lengths,
    value_up,
    output_weight,
    residual,
    norm_gain,
    routed_experts,
    route_weights,
    gate_weight,
    up_weight,
    down_weight,
):
    swap = [(0, 1), (1, 0)]
    role, x, lane = (lax.axis_index(name) for name in ("role", "x", "tp"))

    sent = lax.dynamic_slice_in_dim(routed_experts, (role * X + x) * ROWBLK, ROWBLK, 0).T
    block = (role * TP + lane) * ROWBLK
    routed = lax.dynamic_slice_in_dim(routed_experts, block, ROWBLK, 0).T
    weights = lax.dynamic_slice_in_dim(route_weights, block, ROWBLK, 0).T
    pick, high, low = local_call(
        route_kernel,
        (shape((X * MOST, ROWBLK)), shape((Z * 32, 128)), shape((Z * 32, 128))),
        sent,
        routed,
        weights,
        scratch=(pltpu.VMEM((EXPERTS, ROWBLK), F32), pltpu.VMEM((EXPERTS, ROWBLK), F32)),
    )

    heads = queries.shape[1]
    own_heads = heads // MEMBERS
    width = output_weight.shape[1] + residual.shape[1] // ROLE
    attended, payload = local_call(
        attend_kernel,
        (shape((heads, LAT)), shape((COLS, width))),
        lengths,
        queries,
        latent_cache.swapaxes(1, 2),
        output_weight,
        residual,
        scratch=(
            pltpu.VMEM(queries.shape[1:], BF16),
            pltpu.VMEM(latent_cache.shape[:0:-1], BF16),
            pltpu.SemaphoreType.DMA((4,)),
        ),
        smem=(0,),
        hbm=(1, 2, 3, 4),
        vmem=ALL_VMEM,
    )
    attended, late_value, late_weight = lax.optimization_barrier(
        (attended, value_up, output_weight)
    )
    value_blocks, weight_rows = preload(late_value, late_weight)
    attended = attended.reshape(MEMBERS, own_heads, LAT)
    regrouped = exchange(attended, ("role", "tp"), HEAD_ORDER)
    values = local_call(
        value_kernel,
        shape((Z, MEMBERS, own_heads * 128)),
        regrouped.reshape(MEMBERS * own_heads, LAT),
        value_blocks,
    )
    right, left = ([(i, (i + step) % X) for i in range(X)] for step in (1, X - 1))
    near = lax.ppermute(payload, "x", right)
    payloads = [lax.ppermute(near, "x", right), near, lax.ppermute(payload, "x", left)]
    gathered = exchange(values, "z", z_order(VALUE_FIRST))
    projected = local_call(
        project_kernel,
        shape((MEMBERS, 32, 128)),
        gathered.reshape(Z * MEMBERS, own_heads * 128),
        weight_rows,
        *payloads,
    )
    residual_tile = local_call(
        residual_kernel, shape((32, 128), F32), residual, *payloads
    )
    head_parts = exchange(projected, ("role", "tp"), HEAD_ORDER)
    hidden, own = local_call(
        hidden_kernel, (shape((Z, 32, 128)), shape((32, 128))), head_parts, residual_tile
    )

    gain_rows = norm_gain.reshape(TP, 1, PLANE)
    own_expert = (gate_weight[0], up_weight[0], down_weight[0])
    peer_expert = [lax.ppermute(weight, "role", swap) for weight in own_expert]
    hidden = exchange(hidden, "z", z_order(HIDDEN_FIRST))
    outbound = local_call(
        dispatch_kernel, shape((X * TP, MOST, PLANE)), hidden, pick
    )
    own = lax.ppermute(
        own, ("x", "tp"), [(a * TP + b, b * TP + a) for a in range(X) for b in range(TP)]
    )
    arrived = exchange(outbound, ("x", "tp"), PLANE_ORDER)
    arrived, own = lax.optimization_barrier((arrived, own))
    partial = local_call(
        expert_kernel,
        shape((X * TP, MOST, PLANE)),
        arrived,
        gain_rows,
        *own_expert,
        *peer_expert,
    )
    hidden_parts = exchange(partial, ("x", "tp"), PLANE_ORDER)
    columns = local_call(columns_kernel, shape((Z, 32, 128)), hidden_parts)
    returned = exchange(columns, "z", z_order(RETURN_FIRST))
    return local_call(
        combine_kernel,
        shape((COLS, ROWBLK)),
        returned.reshape(Z * 32, 128),
        high,
        low,
        own,
    )


def solution(mesh):
    grp = ("x", "z")
    fine = Mesh(mesh.devices.reshape(ROLE, X, Z, TP), ("role", "x", "z", "tp"))
    return jax.shard_map(
        shards,
        mesh=fine,
        in_specs=(
            P(("role",) + grp + ("tp",), None, None),
            P(("role",) + grp + ("tp",), None, None),
            P(("role",) + grp + ("tp",)),
            P(("role", "tp"), None, None),
            P(grp, ("role", "tp")),
            P(grp, None),
            P(),
            P(),
            P(),
            P(grp, None, ("role", "tp")),
            P(grp, None, ("role", "tp")),
            P(grp, ("role", "tp"), None),
        ),
        out_specs=P(grp, ("role", "tp")),
        check_vma=False,
    )
```

```python
import jax
import jax.numpy as jnp
from jax import lax
from jax.experimental import pallas as pl
from jax.experimental.pallas import tpu as pltpu
from jax.sharding import Mesh
from jax.sharding import PartitionSpec as P

LAT = 512
SOFTMAX_SCALE = 192.0 ** (-0.5)
NORM_EPS = 1e-06

ROLE, X, Z, TP = 2, 4, 16, 4
MEMBERS = ROLE * TP
ROWBLK = 64
MOST = 16
EXPERTS = 64
COLS = 56
WIDTH = 3584
PLANE = Z * COLS
HALF = 64

VALUE_FIRST, HIDDEN_FIRST, RETURN_FIRST = 8, 4, 8
HEAD_ROLE_FIRST, HEAD_TP_FIRST = 1, 2
PLANE_X_FIRST, PLANE_TP_FIRST = 2, 2


def z_order(first):
    return [(i + first) % Z for i in range(Z)]


def z_places(first):
    return [(z - first) % Z for z in range(Z)]


HEAD_ORDER = [
    (role + HEAD_ROLE_FIRST) % ROLE * TP + (lane + HEAD_TP_FIRST) % TP
    for role in range(ROLE)
    for lane in range(TP)
]
PLANE_ORDER = [
    (x + PLANE_X_FIRST) % X * TP + (lane + PLANE_TP_FIRST) % TP
    for x in range(X)
    for lane in range(TP)
]
HEAD_AT = [HEAD_ORDER.index(i) for i in range(MEMBERS)]
PLANE_AT = [[PLANE_ORDER.index(x * TP + lane) for lane in range(TP)] for x in range(X)]

F32 = jnp.float32
BF16 = jnp.bfloat16
VMEM_LIMIT = 16 * 1024 * 1024
ALL_VMEM = 60 * 1024 * 1024


def nt_dot(a, b):
    return lax.dot_general(a, b, (((1,), (1,)), ((), ())), preferred_element_type=F32)


def nn_dot(a, b):
    return lax.dot_general(a, b, (((1,), (0,)), ((), ())), preferred_element_type=F32)


def local_call(
    body, out_shape, *args, scratch=(), smem=(), hbm=(), out_hbm=(), vmem=VMEM_LIMIT
):
    def space(i, smem, hbm):
        return pltpu.SMEM if i in smem else pltpu.HBM if i in hbm else pltpu.VMEM

    many = isinstance(out_shape, tuple)
    outs = [
        pl.BlockSpec(memory_space=space(i, (), out_hbm))
        for i in range(len(out_shape) if many else 1)
    ]
    return pl.pallas_call(
        body,
        out_shape=out_shape,
        in_specs=[pl.BlockSpec(memory_space=space(i, smem, hbm)) for i in range(len(args))],
        out_specs=tuple(outs) if many else outs[0],
        scratch_shapes=list(scratch),
        compiler_params=pltpu.CompilerParams(vmem_limit_bytes=vmem),
    )(*args)


def exchange(chunks, axes, order):
    return lax.all_to_all(chunks, axes, 0, 0, tiled=True, axis_index_groups=[order])


def shape(dims, dtype=BF16):
    return jax.ShapeDtypeStruct(dims, dtype)


def attend_kernel(
    length_ref,
    query_hbm,
    cache_hbm,
    weight_hbm,
    residual_hbm,
    out_ref,
    payload_hbm,
    query_ref,
    cache_ref,
    sems,
):
    depth = weight_hbm.shape[1]
    span = residual_hbm.shape[1] // ROLE
    start = pl.multiple_of(lax.axis_index("role") * span, span)
    copies = [
        pltpu.make_async_copy(cache_hbm.at[0], cache_ref, sems.at[0]),
        pltpu.make_async_copy(query_hbm.at[0], query_ref, sems.at[1]),
        pltpu.make_async_copy(weight_hbm, payload_hbm.at[:, pl.ds(0, depth)], sems.at[2]),
        pltpu.make_async_copy(
            residual_hbm.at[:, pl.ds(start, span)], payload_hbm.at[:, pl.ds(depth, span)], sems.at[3]
        ),
    ]
    for copy in copies:
        copy.start()
    copies[0].wait()
    copies[1].wait()
    scores = nn_dot(query_ref[...], cache_ref[...]) * SOFTMAX_SCALE
    visible = lax.broadcasted_iota(jnp.int32, scores.shape, 1) < length_ref[0]
    scores = jnp.where(visible, scores, -1e30)
    row_max = jnp.max(scores, axis=1, keepdims=True)
    weights = jnp.where(visible, jnp.exp(scores - row_max), 0.0)
    row_total = jnp.sum(weights, axis=1, keepdims=True)
    summed = nt_dot(weights.astype(BF16), cache_ref[:LAT])
    attended = summed / row_total
    heads = attended.shape[0] // MEMBERS
    attended = [attended[i * heads : (i + 1) * heads] for i in HEAD_ORDER]
    out_ref[...] = jnp.concatenate(attended, axis=0).astype(BF16)
    for copy in copies[2:]:
        copy.wait()


def value_kernel(att_ref, value_ref, out_ref):
    heads = value_ref.shape[0]
    att = att_ref[...]
    rows = att.shape[0]
    row_head = lax.broadcasted_iota(jnp.int32, (rows, 256), 0) % heads
    lane_head = lax.broadcasted_iota(jnp.int32, (rows, 256), 1) // 128
    for head in range(0, heads, 2):
        pair = jnp.concatenate([value_ref[head], value_ref[head + 1]], axis=1)
        kept = jnp.where(row_head == head + lane_head, nn_dot(att, pair), 0.0)
        value = jnp.sum(kept.reshape(rows // heads, heads, 256), axis=1)
        value = jnp.concatenate([value[i : i + 1] for i in HEAD_AT], axis=0).astype(BF16)
        out_ref[:, :, head * 128 : (head + 2) * 128] = jnp.broadcast_to(
            value[None], (out_ref.shape[0],) + value.shape
        )


def packed(tile):
    gap = jnp.zeros((ROWBLK // 2, HALF - COLS), F32)
    return jnp.concatenate([tile[: ROWBLK // 2], gap, tile[ROWBLK // 2 :], gap], axis=1)


def by_source(refs):
    for step, ref in zip((0, 2, 3, 1), refs):
        yield lax.rem(lax.axis_index("x") + step, X), ref


def project_kernel(values_ref, *refs):
    weights, out_ref = refs[:X], refs[X]
    depth = values_ref.shape[1]
    values = values_ref[...]
    for x, weight in by_source(weights):
        product = nt_dot(values, weight[:, :depth]).reshape(Z, MEMBERS, COLS)
        lane = lax.rem(x + TP - HEAD_TP_FIRST, TP)
        for role in range(ROLE):
            tile = jnp.concatenate(
                [product[at, role * TP : (role + 1) * TP] for at in z_places(VALUE_FIRST)], axis=0
            )
            out_ref[(role + HEAD_ROLE_FIRST) % ROLE * TP + lane] = packed(tile).astype(BF16)


def residual_kernel(own_ref, *refs):
    payloads, out_ref = refs[: X - 1], refs[X - 1]
    span = ROWBLK * X
    token = lax.broadcasted_iota(jnp.int32, (ROWBLK, span), 0)
    request = lax.broadcasted_iota(jnp.int32, (ROWBLK, span), 1)
    mine = request == token + lax.axis_index("x") * ROWBLK
    start = pl.multiple_of(lax.axis_index("role") * span, span)
    columns = [own_ref[:, pl.ds(start, span)]]
    columns += [payload[:, payload.shape[1] - span :] for payload in payloads]
    total = jnp.zeros((ROWBLK, COLS), F32)
    for x, column in by_source(columns):
        wanted = mine & (x == lax.axis_index("tp"))
        total = total + nt_dot(jnp.where(wanted, 1.0, 0.0).astype(BF16), column)
    out_ref[...] = packed(total)


def hidden_kernel(parts_ref, residual_ref, out_ref):
    total = jnp.sum(parts_ref[...].astype(F32), axis=0)
    total = (residual_ref[...] + total).astype(BF16)
    out_ref[...] = jnp.broadcast_to(total[None], out_ref.shape)


def block_of(ref, block):
    pair = ref[:, pl.ds(pl.multiple_of(block // 2 * (2 * ROWBLK), 2 * ROWBLK), 2 * ROWBLK)]
    return jnp.where(lax.rem(block, 2) == 0, pair[:, :ROWBLK], pair[:, ROWBLK:])


def route_kernel(routed_ref, weight_ref, pick_ref, slots_ref, place_ref, rank_ref):
    role, x, lane = (lax.axis_index(name) for name in ("role", "x", "tp"))
    z = lax.axis_index("z")
    dims = (EXPERTS, ROWBLK)
    expert_ids = lax.broadcasted_iota(jnp.int32, dims, 0)
    earlier = lax.broadcasted_iota(jnp.int32, (ROWBLK, ROWBLK), 0) < lax.broadcasted_iota(
        jnp.int32, (ROWBLK, ROWBLK), 1
    )
    before = jnp.where(earlier, 1.0, 0.0).astype(BF16)
    slots = lax.broadcasted_iota(jnp.int32, (MOST, ROWBLK), 0).astype(F32)

    def ranks(ids):
        named = jnp.zeros(dims, F32)
        for k in range(ids.shape[0]):
            named = named + jnp.where(expert_ids == ids[k : k + 1, :], 1.0, 0.0)
        rank = nn_dot(named.astype(BF16), before)
        return jnp.where(named > 0.5, rank, -1.0)

    rank_ref[...] = ranks(block_of(routed_ref, role * X + x))
    for i in range(X):
        row = rank_ref[pl.ds(i * Z + z, 1), :]
        pick_ref[i * MOST : (i + 1) * MOST, :] = jnp.where(row == slots, 1.0, 0.0).astype(BF16)

    rank_ref[...] = ranks(block_of(routed_ref, role * TP + lane))
    for half in range(2):
        for i in range(Z):
            for pair in range(2):
                expert = (half * 2 + pair) * Z + i
                hit = rank_ref[expert : expert + 1, :] == slots
                rows = pl.ds(z_places(RETURN_FIRST)[i] * 32 + pair * MOST, MOST)
                lanes = pl.ds(half * HALF, ROWBLK)
                place_ref[rows, lanes] = jnp.where(hit, 1.0, 0.0).astype(BF16)

    span = ROWBLK * X
    start = pl.multiple_of(role * span, span)
    mine = routed_ref[:, pl.ds(start, span)] == x * Z + z
    named = jnp.where(mine, 1.0, 0.0)
    weights = jnp.sum(jnp.where(mine, weight_ref[:, pl.ds(start, span)], 0.0), axis=0, keepdims=True)
    source = lax.broadcasted_iota(jnp.int32, (span, span), 0)
    request = lax.broadcasted_iota(jnp.int32, (span, span), 1)
    inside = (source < request) & (source // ROWBLK == request // ROWBLK)
    rank = nn_dot(named.astype(BF16), jnp.where(inside, 1.0, 0.0).astype(BF16))
    rank = jnp.sum(rank, axis=0, keepdims=True)
    chosen = jnp.sum(named, axis=0, keepdims=True)
    rank = jnp.where(chosen > 0.5, rank, -1.0)
    slot = lax.broadcasted_iota(jnp.int32, (X * MOST, span), 0)
    token = lax.broadcasted_iota(jnp.int32, (X * MOST, span), 1)
    hit = (rank == lax.rem(slot, MOST).astype(F32)) & (token // ROWBLK == slot // MOST)
    weight = jnp.sum(jnp.where(hit, weights, 0.0), axis=1, keepdims=True)
    first = jnp.sum(jnp.where(hit, named[:1], 0.0), axis=1, keepdims=True)
    column = lax.broadcasted_iota(jnp.int32, slots_ref.shape, 1)
    slots_ref[...] = jnp.where(column == 0, weight, first)


def dispatch_kernel(parts_ref, pick_ref, out_ref):
    parts = [parts_ref[at].astype(F32) for at in z_places(HIDDEN_FIRST)]
    hidden = jnp.concatenate(
        [
            jnp.concatenate([part[:, start : start + COLS] for part in parts], axis=1)
            for start in (0, HALF)
        ],
        axis=0,
    ).astype(BF16)
    rows = nn_dot(pick_ref[...], hidden).astype(BF16)
    for x in range(X):
        piece = rows[x * MOST : (x + 1) * MOST]
        for lane in range(TP):
            out_ref[PLANE_AT[x][lane]] = piece


def expert_kernel(arrived_ref, gain_ref, slots_ref, *refs):
    own_refs, peer_refs, out_ref = refs[:3], refs[3:6], refs[6]
    rows = X * MOST
    total = jnp.zeros((rows, 1), F32)
    values, scaled = [], []
    for lane in range(TP):
        value = jnp.concatenate(
            [arrived_ref[PLANE_AT[x][lane]] for x in range(X)], axis=0
        ).astype(F32)
        total = total + jnp.sum(value * value, axis=1, keepdims=True)
        values.append(value)
        scaled.append((value * gain_ref[lane]).astype(BF16))

    def hidden_sums(refs):
        sums = jnp.zeros((rows, 256), F32)
        for lane in range(TP):
            depth = pl.ds(lane * PLANE, PLANE)
            both = jnp.concatenate([refs[0][depth], refs[1][depth]], axis=1)
            sums = sums + nn_dot(scaled[lane], both)
        return sums

    own, peer = hidden_sums(own_refs), hidden_sums(peer_refs)
    inverse = lax.rsqrt(total / WIDTH + NORM_EPS)

    def activate(both):
        both = both * inverse
        gate, up = both[:, :128], both[:, 128:]
        return (gate / (1.0 + jnp.exp(-gate)) * up).astype(BF16)

    activated = jnp.concatenate([activate(own), activate(peer)], axis=1)
    weight = slots_ref[:, 0:1]
    first = slots_ref[:, 1:2] * jnp.where(lax.axis_index("tp") == 0, 1.0, 0.0)
    for x in range(X):
        lanes = slice(x * PLANE, (x + 1) * PLANE)
        down = jnp.concatenate([own_refs[2][:, lanes], peer_refs[2][:, lanes]], axis=0)
        product = (nn_dot(activated, down) * weight + values[x] * first).astype(BF16)
        for lane in range(TP):
            out_ref[PLANE_AT[x][lane]] = product[lane * MOST : (lane + 1) * MOST]


def columns_kernel(parts_ref, out_ref):
    summed = []
    for x in range(X):
        total = parts_ref[PLANE_AT[x][0]].astype(F32)
        for lane in range(1, TP):
            total = total + parts_ref[PLANE_AT[x][lane]].astype(F32)
        summed.append(total)
    low = jnp.concatenate(summed[:2], axis=0)
    high = jnp.concatenate(summed[2:], axis=0)
    gap = jnp.zeros((32, HALF - COLS), F32)
    for z in range(Z):
        cut = slice(z * COLS, (z + 1) * COLS)
        out_ref[z_places(RETURN_FIRST)[z]] = jnp.concatenate([low[:, cut], gap, high[:, cut], gap], axis=1).astype(BF16)


def combine_kernel(returned_ref, place_ref, out_ref):
    dims = (((0,), (0,)), ((), ()))
    mixed = lax.dot_general(
        returned_ref[...], place_ref[...], dims, preferred_element_type=F32
    )
    mixed = mixed[:COLS, :ROWBLK] + mixed[HALF : HALF + COLS, HALF : HALF + ROWBLK]
    out_ref[...] = mixed.astype(BF16)


def preload_kernel(*refs):
    count = (len(refs) - 1) // 2
    sems = refs[-1]
    copies = [
        pltpu.make_async_copy(refs[i], refs[count + i], sems.at[i]) for i in range(count)
    ]
    for copy in copies:
        copy.start()
    for copy in copies:
        copy.wait()


def preload(*arrays):
    return local_call(
        preload_kernel,
        tuple(shape(array.shape, array.dtype) for array in arrays),
        *arrays,
        scratch=(pltpu.SemaphoreType.DMA((len(arrays),)),),
        hbm=range(len(arrays)),
    )


def shards(
    queries,
    latent_cache,
    lengths,
    value_up,
    output_weight,
    residual,
    norm_gain,
    routed_experts,
    route_weights,
    gate_weight,
    up_weight,
    down_weight,
):
    swap = [(0, 1), (1, 0)]
    pick, slots, places = local_call(
        route_kernel,
        (shape((X * MOST, ROWBLK)), shape((X * MOST, 128), F32), shape((Z * 32, 128))),
        routed_experts.T,
        route_weights.T,
        scratch=(pltpu.VMEM((EXPERTS, ROWBLK), F32),),
    )

    heads = queries.shape[1]
    own_heads = heads // MEMBERS
    width = output_weight.shape[1] + residual.shape[1] // ROLE
    attended, payload = local_call(
        attend_kernel,
        (shape((heads, LAT)), shape((COLS, width))),
        lengths,
        queries,
        latent_cache.swapaxes(1, 2),
        output_weight,
        residual,
        scratch=(
            pltpu.VMEM(queries.shape[1:], BF16),
            pltpu.VMEM(latent_cache.shape[:0:-1], BF16),
            pltpu.SemaphoreType.DMA((4,)),
        ),
        smem=(0,),
        hbm=(1, 2, 3, 4),
        vmem=ALL_VMEM,
    )
    attended, late_value, late_weight = lax.optimization_barrier(
        (attended, value_up, output_weight)
    )
    value_blocks, weight_rows = preload(late_value, late_weight)
    attended = attended.reshape(MEMBERS, own_heads, LAT)
    regrouped = exchange(attended, ("role", "tp"), HEAD_ORDER)
    values = local_call(
        value_kernel,
        shape((Z, MEMBERS, own_heads * 128)),
        regrouped.reshape(MEMBERS * own_heads, LAT),
        value_blocks,
    )
    right, left = ([(i, (i + step) % X) for i in range(X)] for step in (1, X - 1))
    near = lax.ppermute(payload, "x", right)
    payloads = [lax.ppermute(near, "x", right), near, lax.ppermute(payload, "x", left)]
    gathered = exchange(values, "z", z_order(VALUE_FIRST))
    projected = local_call(
        project_kernel,
        shape((MEMBERS, 32, 128)),
        gathered.reshape(Z * MEMBERS, own_heads * 128),
        weight_rows,
        *payloads,
    )
    residual_tile = local_call(
        residual_kernel, shape((32, 128), F32), residual, *payloads
    )
    head_parts = exchange(projected, ("role", "tp"), HEAD_ORDER)
    hidden = local_call(hidden_kernel, shape((Z, 32, 128)), head_parts, residual_tile)

    gain_rows = norm_gain.reshape(TP, 1, PLANE)
    own_expert = (gate_weight[0], up_weight[0], down_weight[0])
    peer_expert = [lax.ppermute(weight, "role", swap) for weight in own_expert]
    hidden = exchange(hidden, "z", z_order(HIDDEN_FIRST))
    outbound = local_call(
        dispatch_kernel, shape((X * TP, MOST, PLANE)), hidden, pick
    )
    arrived = exchange(outbound, ("x", "tp"), PLANE_ORDER)
    partial = local_call(
        expert_kernel,
        shape((X * TP, MOST, PLANE)),
        arrived,
        gain_rows,
        slots,
        *own_expert,
        *peer_expert,
    )
    hidden_parts = exchange(partial, ("x", "tp"), PLANE_ORDER)
    columns = local_call(columns_kernel, shape((Z, 32, 128)), hidden_parts)
    returned = exchange(columns, "z", z_order(RETURN_FIRST))
    return local_call(
        combine_kernel,
        shape((COLS, ROWBLK)),
        returned.reshape(Z * 32, 128),
        places,
    )


def solution(mesh):
    grp = ("x", "z")
    fine = Mesh(mesh.devices.reshape(ROLE, X, Z, TP), ("role", "x", "z", "tp"))
    return jax.shard_map(
        shards,
        mesh=fine,
        in_specs=(
            P(("role",) + grp + ("tp",), None, None),
            P(("role",) + grp + ("tp",), None, None),
            P(("role",) + grp + ("tp",)),
            P(("role", "tp"), None, None),
            P(grp, ("role", "tp")),
            P(grp, None),
            P(),
            P(),
            P(),
            P(grp, None, ("role", "tp")),
            P(grp, None, ("role", "tp")),
            P(grp, ("role", "tp"), None),
        ),
        out_specs=P(grp, ("role", "tp")),
        check_vma=False,
    )
```

```python
import jax
import jax.numpy as jnp
from jax import lax
from jax.experimental import pallas as pl
from jax.experimental.pallas import tpu as pltpu
from jax.sharding import Mesh
from jax.sharding import PartitionSpec as P

LAT = 512
SOFTMAX_SCALE = 192.0 ** (-0.5)
NORM_EPS = 1e-06

ROLE, X, Z, TP = 2, 4, 16, 4
MEMBERS = ROLE * TP
ROWBLK = 64
MOST = 16
EXPERTS = 64
COLS = 56
WIDTH = 3584
PLANE = Z * COLS
HALF = 64

VALUE_FIRST, HIDDEN_FIRST, RETURN_FIRST = 8, 4, 8
HEAD_ROLE_FIRST, HEAD_TP_FIRST = 1, 2
PLANE_X_FIRST, PLANE_TP_FIRST = 2, 2


def z_order(first):
    return [(i + first) % Z for i in range(Z)]


def z_places(first):
    return [(z - first) % Z for z in range(Z)]


HEAD_ORDER = [
    (role + HEAD_ROLE_FIRST) % ROLE * TP + (lane + HEAD_TP_FIRST) % TP
    for role in range(ROLE)
    for lane in range(TP)
]
PLANE_ORDER = [
    (x + PLANE_X_FIRST) % X * TP + (lane + PLANE_TP_FIRST) % TP
    for x in range(X)
    for lane in range(TP)
]
HEAD_AT = [HEAD_ORDER.index(i) for i in range(MEMBERS)]
PLANE_AT = [[PLANE_ORDER.index(x * TP + lane) for lane in range(TP)] for x in range(X)]

F32 = jnp.float32
BF16 = jnp.bfloat16
VMEM_LIMIT = 16 * 1024 * 1024
ALL_VMEM = 60 * 1024 * 1024


def nt_dot(a, b):
    return lax.dot_general(a, b, (((1,), (1,)), ((), ())), preferred_element_type=F32)


def nn_dot(a, b):
    return lax.dot_general(a, b, (((1,), (0,)), ((), ())), preferred_element_type=F32)


def local_call(
    body, out_shape, *args, scratch=(), smem=(), hbm=(), out_hbm=(), vmem=VMEM_LIMIT
):
    def space(i, smem, hbm):
        return pltpu.SMEM if i in smem else pltpu.HBM if i in hbm else pltpu.VMEM

    many = isinstance(out_shape, tuple)
    outs = [
        pl.BlockSpec(memory_space=space(i, (), out_hbm))
        for i in range(len(out_shape) if many else 1)
    ]
    return pl.pallas_call(
        body,
        out_shape=out_shape,
        in_specs=[pl.BlockSpec(memory_space=space(i, smem, hbm)) for i in range(len(args))],
        out_specs=tuple(outs) if many else outs[0],
        scratch_shapes=list(scratch),
        compiler_params=pltpu.CompilerParams(vmem_limit_bytes=vmem),
    )(*args)


def exchange(chunks, axes, order):
    return lax.all_to_all(chunks, axes, 0, 0, tiled=True, axis_index_groups=[order])


def whole(dims):
    return pl.BlockSpec(dims, lambda i: (0,) * len(dims))


def shape(dims, dtype=BF16):
    return jax.ShapeDtypeStruct(dims, dtype)


def attend_kernel(
    length_ref, query_ref, cache_ref, weight_ref, residual_ref, out_ref, payload_ref
):
    depth = weight_ref.shape[1]
    span = residual_ref.shape[1] // ROLE
    start = pl.multiple_of(lax.axis_index("role") * span, span)
    payload_ref[:, :depth] = weight_ref[...]
    payload_ref[:, depth:] = residual_ref[:, pl.ds(start, span)]
    cache = cache_ref[0]
    scores = nn_dot(query_ref[0], cache) * SOFTMAX_SCALE
    visible = lax.broadcasted_iota(jnp.int32, scores.shape, 1) < length_ref[0]
    scores = jnp.where(visible, scores, -1e30)
    row_max = jnp.max(scores, axis=1, keepdims=True)
    weights = jnp.where(visible, jnp.exp(scores - row_max), 0.0)
    row_total = jnp.sum(weights, axis=1, keepdims=True)
    summed = nt_dot(weights.astype(BF16), cache[:LAT])
    attended = summed / row_total
    heads = attended.shape[0] // MEMBERS
    attended = [attended[i * heads : (i + 1) * heads] for i in HEAD_ORDER]
    out_ref[...] = jnp.concatenate(attended, axis=0).astype(BF16)


def value_kernel(att_ref, value_ref, out_ref):
    heads = value_ref.shape[0]
    att = att_ref[...]
    rows = att.shape[0]
    row_head = lax.broadcasted_iota(jnp.int32, (rows, 256), 0) % heads
    lane_head = lax.broadcasted_iota(jnp.int32, (rows, 256), 1) // 128
    for head in range(0, heads, 2):
        pair = jnp.concatenate([value_ref[head], value_ref[head + 1]], axis=1)
        kept = jnp.where(row_head == head + lane_head, nn_dot(att, pair), 0.0)
        value = jnp.sum(kept.reshape(rows // heads, heads, 256), axis=1)
        value = jnp.concatenate([value[i : i + 1] for i in HEAD_AT], axis=0).astype(BF16)
        out_ref[:, :, head * 128 : (head + 2) * 128] = jnp.broadcast_to(
            value[None], (out_ref.shape[0],) + value.shape
        )


def packed(tile):
    gap = jnp.zeros((ROWBLK // 2, HALF - COLS), F32)
    return jnp.concatenate([tile[: ROWBLK // 2], gap, tile[ROWBLK // 2 :], gap], axis=1)


def by_source(refs):
    for step, ref in zip((0, 2, 3, 1), refs):
        yield lax.rem(lax.axis_index("x") + step, X), ref


def project_kernel(values_ref, *refs):
    weights, out_ref = refs[:X], refs[X]
    depth = values_ref.shape[1]
    values = values_ref[...]
    for x, weight in by_source(weights):
        product = nt_dot(values, weight[:, :depth]).reshape(Z, MEMBERS, COLS)
        lane = lax.rem(x + TP - HEAD_TP_FIRST, TP)
        for role in range(ROLE):
            tile = jnp.concatenate(
                [product[at, role * TP : (role + 1) * TP] for at in z_places(VALUE_FIRST)], axis=0
            )
            out_ref[(role + HEAD_ROLE_FIRST) % ROLE * TP + lane] = packed(tile).astype(BF16)


def residual_kernel(own_ref, *refs):
    payloads, out_ref = refs[: X - 1], refs[X - 1]
    span = ROWBLK * X
    token = lax.broadcasted_iota(jnp.int32, (ROWBLK, span), 0)
    request = lax.broadcasted_iota(jnp.int32, (ROWBLK, span), 1)
    mine = request == token + lax.axis_index("x") * ROWBLK
    start = pl.multiple_of(lax.axis_index("role") * span, span)
    columns = [own_ref[:, pl.ds(start, span)]]
    columns += [payload[:, payload.shape[1] - span :] for payload in payloads]
    total = jnp.zeros((ROWBLK, COLS), F32)
    for x, column in by_source(columns):
        wanted = mine & (x == lax.axis_index("tp"))
        total = total + nt_dot(jnp.where(wanted, 1.0, 0.0).astype(BF16), column)
    out_ref[...] = packed(total)


def hidden_kernel(parts_ref, residual_ref, out_ref):
    total = jnp.sum(parts_ref[...].astype(F32), axis=0)
    total = (residual_ref[...] + total).astype(BF16)
    out_ref[...] = jnp.broadcast_to(total[None], out_ref.shape)


def block_of(ref, block):
    pair = ref[:, pl.ds(pl.multiple_of(block // 2 * (2 * ROWBLK), 2 * ROWBLK), 2 * ROWBLK)]
    return jnp.where(lax.rem(block, 2) == 0, pair[:, :ROWBLK], pair[:, ROWBLK:])


def route_kernel(routed_ref, weight_ref, pick_ref, slots_ref, place_ref, rank_ref):
    role, x, lane = (lax.axis_index(name) for name in ("role", "x", "tp"))
    z = lax.axis_index("z")
    dims = (EXPERTS, ROWBLK)
    expert_ids = lax.broadcasted_iota(jnp.int32, dims, 0)
    earlier = lax.broadcasted_iota(jnp.int32, (ROWBLK, ROWBLK), 0) < lax.broadcasted_iota(
        jnp.int32, (ROWBLK, ROWBLK), 1
    )
    before = jnp.where(earlier, 1.0, 0.0).astype(BF16)
    slots = lax.broadcasted_iota(jnp.int32, (MOST, ROWBLK), 0).astype(F32)

    def ranks(ids):
        named = jnp.zeros(dims, F32)
        for k in range(ids.shape[0]):
            named = named + jnp.where(expert_ids == ids[k : k + 1, :], 1.0, 0.0)
        rank = nn_dot(named.astype(BF16), before)
        return jnp.where(named > 0.5, rank, -1.0)

    rank_ref[...] = ranks(block_of(routed_ref, role * X + x))
    for i in range(X):
        row = rank_ref[pl.ds(i * Z + z, 1), :]
        pick_ref[i * MOST : (i + 1) * MOST, :] = jnp.where(row == slots, 1.0, 0.0).astype(BF16)

    rank_ref[...] = ranks(block_of(routed_ref, role * TP + lane))
    for half in range(2):
        for i in range(Z):
            for pair in range(2):
                expert = (half * 2 + pair) * Z + i
                hit = rank_ref[expert : expert + 1, :] == slots
                rows = pl.ds(z_places(RETURN_FIRST)[i] * 32 + pair * MOST, MOST)
                lanes = pl.ds(half * HALF, ROWBLK)
                place_ref[rows, lanes] = jnp.where(hit, 1.0, 0.0).astype(BF16)

    span = ROWBLK * X
    start = pl.multiple_of(role * span, span)
    mine = routed_ref[:, pl.ds(start, span)] == x * Z + z
    named = jnp.where(mine, 1.0, 0.0)
    weights = jnp.sum(jnp.where(mine, weight_ref[:, pl.ds(start, span)], 0.0), axis=0, keepdims=True)
    source = lax.broadcasted_iota(jnp.int32, (span, span), 0)
    request = lax.broadcasted_iota(jnp.int32, (span, span), 1)
    inside = (source < request) & (source // ROWBLK == request // ROWBLK)
    rank = nn_dot(named.astype(BF16), jnp.where(inside, 1.0, 0.0).astype(BF16))
    rank = jnp.sum(rank, axis=0, keepdims=True)
    chosen = jnp.sum(named, axis=0, keepdims=True)
    rank = jnp.where(chosen > 0.5, rank, -1.0)
    slot = lax.broadcasted_iota(jnp.int32, (X * MOST, span), 0)
    token = lax.broadcasted_iota(jnp.int32, (X * MOST, span), 1)
    hit = (rank == lax.rem(slot, MOST).astype(F32)) & (token // ROWBLK == slot // MOST)
    weight = jnp.sum(jnp.where(hit, weights, 0.0), axis=1, keepdims=True)
    first = jnp.sum(jnp.where(hit, named[:1], 0.0), axis=1, keepdims=True)
    column = lax.broadcasted_iota(jnp.int32, slots_ref.shape, 1)
    slots_ref[...] = jnp.where(column == 0, weight, first)


def dispatch_kernel(parts_ref, pick_ref, out_ref):
    parts = [parts_ref[at].astype(F32) for at in z_places(HIDDEN_FIRST)]
    hidden = jnp.concatenate(
        [
            jnp.concatenate([part[:, start : start + COLS] for part in parts], axis=1)
            for start in (0, HALF)
        ],
        axis=0,
    ).astype(BF16)
    rows = nn_dot(pick_ref[...], hidden).astype(BF16)
    for x in range(X):
        piece = rows[x * MOST : (x + 1) * MOST]
        for lane in range(TP):
            out_ref[PLANE_AT[x][lane]] = piece


def expert_kernel(arrived_ref, gain_ref, slots_ref, *refs):
    own_refs, peer_refs, out_ref = refs[:3], refs[3:6], refs[6]
    rows = X * MOST
    total = jnp.zeros((rows, 1), F32)
    values, scaled = [], []
    for lane in range(TP):
        value = jnp.concatenate(
            [arrived_ref[PLANE_AT[x][lane]] for x in range(X)], axis=0
        ).astype(F32)
        total = total + jnp.sum(value * value, axis=1, keepdims=True)
        values.append(value)
        scaled.append((value * gain_ref[lane]).astype(BF16))

    def hidden_sums(refs):
        sums = jnp.zeros((rows, 256), F32)
        for lane in range(TP):
            depth = pl.ds(lane * PLANE, PLANE)
            both = jnp.concatenate([refs[0][depth], refs[1][depth]], axis=1)
            sums = sums + nn_dot(scaled[lane], both)
        return sums

    own, peer = hidden_sums(own_refs), hidden_sums(peer_refs)
    inverse = lax.rsqrt(total / WIDTH + NORM_EPS)

    def activate(both):
        both = both * inverse
        gate, up = both[:, :128], both[:, 128:]
        return (gate / (1.0 + jnp.exp(-gate)) * up).astype(BF16)

    activated = jnp.concatenate([activate(own), activate(peer)], axis=1)
    weight = slots_ref[:, 0:1]
    first = slots_ref[:, 1:2] * jnp.where(lax.axis_index("tp") == 0, 1.0, 0.0)
    for x in range(X):
        lanes = slice(x * PLANE, (x + 1) * PLANE)
        down = jnp.concatenate([own_refs[2][:, lanes], peer_refs[2][:, lanes]], axis=0)
        product = (nn_dot(activated, down) * weight + values[x] * first).astype(BF16)
        for lane in range(TP):
            out_ref[PLANE_AT[x][lane]] = product[lane * MOST : (lane + 1) * MOST]


def columns_kernel(parts_ref, out_ref):
    summed = []
    for x in range(X):
        total = parts_ref[PLANE_AT[x][0]].astype(F32)
        for lane in range(1, TP):
            total = total + parts_ref[PLANE_AT[x][lane]].astype(F32)
        summed.append(total)
    low = jnp.concatenate(summed[:2], axis=0)
    high = jnp.concatenate(summed[2:], axis=0)
    gap = jnp.zeros((32, HALF - COLS), F32)
    for z in range(Z):
        cut = slice(z * COLS, (z + 1) * COLS)
        out_ref[z_places(RETURN_FIRST)[z]] = jnp.concatenate([low[:, cut], gap, high[:, cut], gap], axis=1).astype(BF16)


def combine_kernel(returned_ref, place_ref, out_ref):
    dims = (((0,), (0,)), ((), ()))
    mixed = lax.dot_general(
        returned_ref[...], place_ref[...], dims, preferred_element_type=F32
    )
    mixed = mixed[:COLS, :ROWBLK] + mixed[HALF : HALF + COLS, HALF : HALF + ROWBLK]
    out_ref[...] = mixed.astype(BF16)


def preload_kernel(*refs):
    count = (len(refs) - 1) // 2
    sems = refs[-1]
    copies = [
        pltpu.make_async_copy(refs[i], refs[count + i], sems.at[i]) for i in range(count)
    ]
    for copy in copies:
        copy.start()
    for copy in copies:
        copy.wait()


def preload(*arrays):
    return local_call(
        preload_kernel,
        tuple(shape(array.shape, array.dtype) for array in arrays),
        *arrays,
        scratch=(pltpu.SemaphoreType.DMA((len(arrays),)),),
        hbm=range(len(arrays)),
    )


def shards(
    queries,
    latent_cache,
    lengths,
    value_up,
    output_weight,
    residual,
    norm_gain,
    routed_experts,
    route_weights,
    gate_weight,
    up_weight,
    down_weight,
):
    swap = [(0, 1), (1, 0)]
    pick, slots, places = local_call(
        route_kernel,
        (shape((X * MOST, ROWBLK)), shape((X * MOST, 128), F32), shape((Z * 32, 128))),
        routed_experts.T,
        route_weights.T,
        scratch=(pltpu.VMEM((EXPERTS, ROWBLK), F32),),
    )

    heads = queries.shape[1]
    own_heads = heads // MEMBERS
    width = output_weight.shape[1] + residual.shape[1] // ROLE
    cache = latent_cache.swapaxes(1, 2)
    attended, payload = pl.pallas_call(
        attend_kernel,
        grid=(1,),
        out_shape=(shape((heads, LAT)), shape((COLS, width))),
        in_specs=[pl.BlockSpec(memory_space=pltpu.SMEM)]
        + [whole(array.shape) for array in (queries, cache, output_weight, residual)],
        out_specs=(whole((heads, LAT)), whole((COLS, width))),
        compiler_params=pltpu.CompilerParams(vmem_limit_bytes=ALL_VMEM),
    )(lengths, queries, cache, output_weight, residual)
    attended, late_value = lax.optimization_barrier((attended, value_up))
    (value_blocks,) = preload(late_value)
    attended = attended.reshape(MEMBERS, own_heads, LAT)
    regrouped = exchange(attended, ("role", "tp"), HEAD_ORDER)
    values = local_call(
        value_kernel,
        shape((Z, MEMBERS, own_heads * 128)),
        regrouped.reshape(MEMBERS * own_heads, LAT),
        value_blocks,
    )
    right, left = ([(i, (i + step) % X) for i in range(X)] for step in (1, X - 1))
    near = lax.ppermute(payload, "x", right)
    payloads = [lax.ppermute(near, "x", right), near, lax.ppermute(payload, "x", left)]
    gathered = exchange(values, "z", z_order(VALUE_FIRST))
    projected = local_call(
        project_kernel,
        shape((MEMBERS, 32, 128)),
        gathered.reshape(Z * MEMBERS, own_heads * 128),
        output_weight,
        *payloads,
    )
    residual_tile = local_call(
        residual_kernel, shape((32, 128), F32), residual, *payloads
    )
    head_parts = exchange(projected, ("role", "tp"), HEAD_ORDER)
    hidden = local_call(hidden_kernel, shape((Z, 32, 128)), head_parts, residual_tile)

    gain_rows = norm_gain.reshape(TP, 1, PLANE)
    own_expert = (gate_weight[0], up_weight[0], down_weight[0])
    peer_expert = [lax.ppermute(weight, "role", swap) for weight in own_expert]
    hidden = exchange(hidden, "z", z_order(HIDDEN_FIRST))
    outbound = local_call(
        dispatch_kernel, shape((X * TP, MOST, PLANE)), hidden, pick
    )
    arrived = exchange(outbound, ("x", "tp"), PLANE_ORDER)
    partial = local_call(
        expert_kernel,
        shape((X * TP, MOST, PLANE)),
        arrived,
        gain_rows,
        slots,
        *own_expert,
        *peer_expert,
    )
    hidden_parts = exchange(partial, ("x", "tp"), PLANE_ORDER)
    columns = local_call(columns_kernel, shape((Z, 32, 128)), hidden_parts)
    returned = exchange(columns, "z", z_order(RETURN_FIRST))
    return local_call(
        combine_kernel,
        shape((COLS, ROWBLK)),
        returned.reshape(Z * 32, 128),
        places,
    )


def solution(mesh):
    grp = ("x", "z")
    fine = Mesh(mesh.devices.reshape(ROLE, X, Z, TP), ("role", "x", "z", "tp"))
    return jax.shard_map(
        shards,
        mesh=fine,
        in_specs=(
            P(("role",) + grp + ("tp",), None, None),
            P(("role",) + grp + ("tp",), None, None),
            P(("role",) + grp + ("tp",)),
            P(("role", "tp"), None, None),
            P(grp, ("role", "tp")),
            P(grp, None),
            P(),
            P(),
            P(),
            P(grp, None, ("role", "tp")),
            P(grp, None, ("role", "tp")),
            P(grp, ("role", "tp"), None),
        ),
        out_specs=P(grp, ("role", "tp")),
        check_vma=False,
    )
```

```python
import jax
import jax.numpy as jnp
from jax import lax
from jax.experimental import pallas as pl
from jax.experimental.pallas import tpu as pltpu
from jax.sharding import Mesh
from jax.sharding import PartitionSpec as P

LAT = 512
SOFTMAX_SCALE = 192.0 ** (-0.5)
NORM_EPS = 1e-06

ROLE, X, Z, TP = 2, 4, 16, 4
MEMBERS = ROLE * TP
ROWBLK = 64
MOST = 16
EXPERTS = 64
COLS = 56
WIDTH = 3584
PLANE = Z * COLS
HALF = 64

VALUE_FIRST, HIDDEN_FIRST, RETURN_FIRST = 8, 4, 8
HEAD_ROLE_FIRST, HEAD_TP_FIRST = 1, 2
PLANE_X_FIRST, PLANE_TP_FIRST = 2, 2


def z_order(first):
    return [(i + first) % Z for i in range(Z)]


def z_places(first):
    return [(z - first) % Z for z in range(Z)]


HEAD_ORDER = [
    (role + HEAD_ROLE_FIRST) % ROLE * TP + (lane + HEAD_TP_FIRST) % TP
    for role in range(ROLE)
    for lane in range(TP)
]
PLANE_ORDER = [
    (x + PLANE_X_FIRST) % X * TP + (lane + PLANE_TP_FIRST) % TP
    for x in range(X)
    for lane in range(TP)
]
HEAD_AT = [HEAD_ORDER.index(i) for i in range(MEMBERS)]
PLANE_AT = [[PLANE_ORDER.index(x * TP + lane) for lane in range(TP)] for x in range(X)]

F32 = jnp.float32
BF16 = jnp.bfloat16
VMEM_LIMIT = 16 * 1024 * 1024
ALL_VMEM = 60 * 1024 * 1024


def nt_dot(a, b):
    return lax.dot_general(a, b, (((1,), (1,)), ((), ())), preferred_element_type=F32)


def nn_dot(a, b):
    return lax.dot_general(a, b, (((1,), (0,)), ((), ())), preferred_element_type=F32)


def local_call(
    body, out_shape, *args, scratch=(), smem=(), hbm=(), out_hbm=(), vmem=VMEM_LIMIT
):
    def space(i, smem, hbm):
        return pltpu.SMEM if i in smem else pltpu.HBM if i in hbm else pltpu.VMEM

    many = isinstance(out_shape, tuple)
    outs = [
        pl.BlockSpec(memory_space=space(i, (), out_hbm))
        for i in range(len(out_shape) if many else 1)
    ]
    return pl.pallas_call(
        body,
        out_shape=out_shape,
        in_specs=[pl.BlockSpec(memory_space=space(i, smem, hbm)) for i in range(len(args))],
        out_specs=tuple(outs) if many else outs[0],
        scratch_shapes=list(scratch),
        compiler_params=pltpu.CompilerParams(vmem_limit_bytes=vmem),
    )(*args)


def exchange(chunks, axes, order):
    return lax.all_to_all(chunks, axes, 0, 0, tiled=True, axis_index_groups=[order])


def whole(dims):
    return pl.BlockSpec(dims, lambda i: (0,) * len(dims))


def shape(dims, dtype=BF16):
    return jax.ShapeDtypeStruct(dims, dtype)


def attend_kernel(
    length_ref, query_ref, cache_ref, weight_ref, residual_ref, out_ref, payload_ref
):
    depth = weight_ref.shape[1]
    span = residual_ref.shape[1] // ROLE
    start = pl.multiple_of(lax.axis_index("role") * span, span)
    payload_ref[:, :depth] = weight_ref[...]
    payload_ref[:, depth:] = residual_ref[:, pl.ds(start, span)]
    cache = cache_ref[0]
    scores = nn_dot(query_ref[0], cache) * SOFTMAX_SCALE
    visible = lax.broadcasted_iota(jnp.int32, scores.shape, 1) < length_ref[0]
    scores = jnp.where(visible, scores, -1e30)
    row_max = jnp.max(scores, axis=1, keepdims=True)
    weights = jnp.where(visible, jnp.exp(scores - row_max), 0.0)
    row_total = jnp.sum(weights, axis=1, keepdims=True)
    summed = nt_dot(weights.astype(BF16), cache[:LAT])
    attended = summed / row_total
    heads = attended.shape[0] // MEMBERS
    attended = [attended[i * heads : (i + 1) * heads] for i in HEAD_ORDER]
    out_ref[...] = jnp.concatenate(attended, axis=0).astype(BF16)


def value_kernel(att_ref, value_ref, out_ref):
    heads = value_ref.shape[0]
    att = att_ref[...]
    rows = att.shape[0]
    row_head = lax.broadcasted_iota(jnp.int32, (rows, 256), 0) % heads
    lane_head = lax.broadcasted_iota(jnp.int32, (rows, 256), 1) // 128
    for head in range(0, heads, 2):
        pair = jnp.concatenate([value_ref[head], value_ref[head + 1]], axis=1)
        kept = jnp.where(row_head == head + lane_head, nn_dot(att, pair), 0.0)
        value = jnp.sum(kept.reshape(rows // heads, heads, 256), axis=1)
        value = jnp.concatenate([value[i : i + 1] for i in HEAD_AT], axis=0).astype(BF16)
        out_ref[:, :, head * 128 : (head + 2) * 128] = jnp.broadcast_to(
            value[None], (out_ref.shape[0],) + value.shape
        )


def packed(tile):
    gap = jnp.zeros((ROWBLK // 2, HALF - COLS), F32)
    return jnp.concatenate([tile[: ROWBLK // 2], gap, tile[ROWBLK // 2 :], gap], axis=1)


def by_source(refs):
    for step, ref in zip((0, 2, 3, 1), refs):
        yield lax.rem(lax.axis_index("x") + step, X), ref


def project_kernel(values_ref, *refs):
    weights, out_ref = refs[:X], refs[X]
    depth = values_ref.shape[1]
    values = values_ref[...]
    for x, weight in by_source(weights):
        product = nt_dot(values, weight[:, :depth]).reshape(Z, MEMBERS, COLS)
        lane = lax.rem(x + TP - HEAD_TP_FIRST, TP)
        for role in range(ROLE):
            tile = jnp.concatenate(
                [product[at, role * TP : (role + 1) * TP] for at in z_places(VALUE_FIRST)], axis=0
            )
            out_ref[(role + HEAD_ROLE_FIRST) % ROLE * TP + lane] = packed(tile).astype(BF16)


def residual_kernel(own_ref, *refs):
    payloads, out_ref = refs[: X - 1], refs[X - 1]
    span = ROWBLK * X
    token = lax.broadcasted_iota(jnp.int32, (ROWBLK, span), 0)
    request = lax.broadcasted_iota(jnp.int32, (ROWBLK, span), 1)
    mine = request == token + lax.axis_index("x") * ROWBLK
    start = pl.multiple_of(lax.axis_index("role") * span, span)
    columns = [own_ref[:, pl.ds(start, span)]]
    columns += [payload[:, payload.shape[1] - span :] for payload in payloads]
    total = jnp.zeros((ROWBLK, COLS), F32)
    for x, column in by_source(columns):
        wanted = mine & (x == lax.axis_index("tp"))
        total = total + nt_dot(jnp.where(wanted, 1.0, 0.0).astype(BF16), column)
    out_ref[...] = packed(total)


def hidden_kernel(parts_ref, residual_ref, out_ref):
    total = jnp.sum(parts_ref[...].astype(F32), axis=0)
    total = (residual_ref[...] + total).astype(BF16)
    out_ref[...] = jnp.broadcast_to(total[None], out_ref.shape)


def block_of(ref, block):
    pair = ref[:, pl.ds(pl.multiple_of(block // 2 * (2 * ROWBLK), 2 * ROWBLK), 2 * ROWBLK)]
    return jnp.where(lax.rem(block, 2) == 0, pair[:, :ROWBLK], pair[:, ROWBLK:])


def route_kernel(routed_ref, weight_ref, pick_ref, slots_ref, place_ref, rank_ref):
    role, x, lane = (lax.axis_index(name) for name in ("role", "x", "tp"))
    z = lax.axis_index("z")
    dims = (EXPERTS, ROWBLK)
    expert_ids = lax.broadcasted_iota(jnp.int32, dims, 0)
    earlier = lax.broadcasted_iota(jnp.int32, (ROWBLK, ROWBLK), 0) < lax.broadcasted_iota(
        jnp.int32, (ROWBLK, ROWBLK), 1
    )
    before = jnp.where(earlier, 1.0, 0.0).astype(BF16)
    slots = lax.broadcasted_iota(jnp.int32, (MOST, ROWBLK), 0).astype(F32)

    def ranks(ids):
        named = jnp.zeros(dims, F32)
        for k in range(ids.shape[0]):
            named = named + jnp.where(expert_ids == ids[k : k + 1, :], 1.0, 0.0)
        rank = nn_dot(named.astype(BF16), before)
        return jnp.where(named > 0.5, rank, -1.0)

    rank_ref[...] = ranks(block_of(routed_ref, role * X + x))
    for i in range(X):
        row = rank_ref[pl.ds(i * Z + z, 1), :]
        pick_ref[i * MOST : (i + 1) * MOST, :] = jnp.where(row == slots, 1.0, 0.0).astype(BF16)

    rank_ref[...] = ranks(block_of(routed_ref, role * TP + lane))
    for half in range(2):
        for i in range(Z):
            for pair in range(2):
                expert = (half * 2 + pair) * Z + i
                hit = rank_ref[expert : expert + 1, :] == slots
                rows = pl.ds(z_places(RETURN_FIRST)[i] * 32 + pair * MOST, MOST)
                lanes = pl.ds(half * HALF, ROWBLK)
                place_ref[rows, lanes] = jnp.where(hit, 1.0, 0.0).astype(BF16)

    span = ROWBLK * X
    start = pl.multiple_of(role * span, span)
    mine = routed_ref[:, pl.ds(start, span)] == x * Z + z
    named = jnp.where(mine, 1.0, 0.0)
    weights = jnp.sum(jnp.where(mine, weight_ref[:, pl.ds(start, span)], 0.0), axis=0, keepdims=True)
    source = lax.broadcasted_iota(jnp.int32, (span, span), 0)
    request = lax.broadcasted_iota(jnp.int32, (span, span), 1)
    inside = (source < request) & (source // ROWBLK == request // ROWBLK)
    rank = nn_dot(named.astype(BF16), jnp.where(inside, 1.0, 0.0).astype(BF16))
    rank = jnp.sum(rank, axis=0, keepdims=True)
    chosen = jnp.sum(named, axis=0, keepdims=True)
    rank = jnp.where(chosen > 0.5, rank, -1.0)
    slot = lax.broadcasted_iota(jnp.int32, (X * MOST, span), 0)
    token = lax.broadcasted_iota(jnp.int32, (X * MOST, span), 1)
    hit = (rank == lax.rem(slot, MOST).astype(F32)) & (token // ROWBLK == slot // MOST)
    weight = jnp.sum(jnp.where(hit, weights, 0.0), axis=1, keepdims=True)
    first = jnp.sum(jnp.where(hit, named[:1], 0.0), axis=1, keepdims=True)
    column = lax.broadcasted_iota(jnp.int32, slots_ref.shape, 1)
    slots_ref[...] = jnp.where(column == 0, weight, first)


def dispatch_kernel(parts_ref, pick_ref, out_ref):
    parts = [parts_ref[at].astype(F32) for at in z_places(HIDDEN_FIRST)]
    hidden = jnp.concatenate(
        [
            jnp.concatenate([part[:, start : start + COLS] for part in parts], axis=1)
            for start in (0, HALF)
        ],
        axis=0,
    ).astype(BF16)
    rows = nn_dot(pick_ref[...], hidden).astype(BF16)
    for x in range(X):
        piece = rows[x * MOST : (x + 1) * MOST]
        for lane in range(TP):
            out_ref[PLANE_AT[x][lane]] = piece


def expert_kernel(arrived_ref, gain_ref, slots_ref, *refs):
    own_refs, peer_refs, out_ref = refs[:3], refs[3:6], refs[6]
    rows = X * MOST
    total = jnp.zeros((rows, 1), F32)
    values, scaled = [], []
    for lane in range(TP):
        value = jnp.concatenate(
            [arrived_ref[PLANE_AT[x][lane]] for x in range(X)], axis=0
        ).astype(F32)
        total = total + jnp.sum(value * value, axis=1, keepdims=True)
        values.append(value)
        scaled.append((value * gain_ref[lane]).astype(BF16))

    def hidden_sums(refs):
        sums = jnp.zeros((rows, 256), F32)
        for lane in range(TP):
            depth = pl.ds(lane * PLANE, PLANE)
            both = jnp.concatenate([refs[0][depth], refs[1][depth]], axis=1)
            sums = sums + nn_dot(scaled[lane], both)
        return sums

    own, peer = hidden_sums(own_refs), hidden_sums(peer_refs)
    inverse = lax.rsqrt(total / WIDTH + NORM_EPS)

    def activate(both):
        both = both * inverse
        gate, up = both[:, :128], both[:, 128:]
        return (gate / (1.0 + jnp.exp(-gate)) * up).astype(BF16)

    activated = jnp.concatenate([activate(own), activate(peer)], axis=1)
    weight = slots_ref[:, 0:1]
    first = slots_ref[:, 1:2] * jnp.where(lax.axis_index("tp") == 0, 1.0, 0.0)
    for x in range(X):
        lanes = slice(x * PLANE, (x + 1) * PLANE)
        down = jnp.concatenate([own_refs[2][:, lanes], peer_refs[2][:, lanes]], axis=0)
        product = (nn_dot(activated, down) * weight + values[x] * first).astype(BF16)
        for lane in range(TP):
            out_ref[PLANE_AT[x][lane]] = product[lane * MOST : (lane + 1) * MOST]


def columns_kernel(parts_ref, out_ref):
    summed = []
    for x in range(X):
        total = parts_ref[PLANE_AT[x][0]].astype(F32)
        for lane in range(1, TP):
            total = total + parts_ref[PLANE_AT[x][lane]].astype(F32)
        summed.append(total)
    low = jnp.concatenate(summed[:2], axis=0)
    high = jnp.concatenate(summed[2:], axis=0)
    gap = jnp.zeros((32, HALF - COLS), F32)
    for z in range(Z):
        cut = slice(z * COLS, (z + 1) * COLS)
        out_ref[z_places(RETURN_FIRST)[z]] = jnp.concatenate([low[:, cut], gap, high[:, cut], gap], axis=1).astype(BF16)


def combine_kernel(returned_ref, place_ref, out_ref):
    dims = (((0,), (0,)), ((), ()))
    mixed = lax.dot_general(
        returned_ref[...], place_ref[...], dims, preferred_element_type=F32
    )
    mixed = mixed[:COLS, :ROWBLK] + mixed[HALF : HALF + COLS, HALF : HALF + ROWBLK]
    out_ref[...] = mixed.astype(BF16)


def preload_kernel(*refs):
    count = (len(refs) - 1) // 2
    sems = refs[-1]
    copies = [
        pltpu.make_async_copy(refs[i], refs[count + i], sems.at[i]) for i in range(count)
    ]
    for copy in copies:
        copy.start()
    for copy in copies:
        copy.wait()


def preload(*arrays):
    return local_call(
        preload_kernel,
        tuple(shape(array.shape, array.dtype) for array in arrays),
        *arrays,
        scratch=(pltpu.SemaphoreType.DMA((len(arrays),)),),
        hbm=range(len(arrays)),
    )


def shards(
    queries,
    latent_cache,
    lengths,
    value_up,
    output_weight,
    residual,
    norm_gain,
    routed_experts,
    route_weights,
    gate_weight,
    up_weight,
    down_weight,
):
    swap = [(0, 1), (1, 0)]
    pick, slots, places = local_call(
        route_kernel,
        (shape((X * MOST, ROWBLK)), shape((X * MOST, 128), F32), shape((Z * 32, 128))),
        routed_experts.T,
        route_weights.T,
        scratch=(pltpu.VMEM((EXPERTS, ROWBLK), F32),),
    )

    heads = queries.shape[1]
    own_heads = heads // MEMBERS
    width = output_weight.shape[1] + residual.shape[1] // ROLE
    cache = latent_cache.swapaxes(1, 2)
    attended, payload = pl.pallas_call(
        attend_kernel,
        grid=(1,),
        out_shape=(shape((heads, LAT)), shape((COLS, width))),
        in_specs=[pl.BlockSpec(memory_space=pltpu.SMEM)]
        + [whole(array.shape) for array in (queries, cache, output_weight, residual)],
        out_specs=(whole((heads, LAT)), whole((COLS, width))),
        compiler_params=pltpu.CompilerParams(vmem_limit_bytes=ALL_VMEM),
    )(lengths, queries, cache, output_weight, residual)
    attended, late_value = lax.optimization_barrier((attended, value_up))
    (value_blocks,) = preload(late_value)
    attended = attended.reshape(MEMBERS, own_heads, LAT)
    regrouped = exchange(attended, ("role", "tp"), HEAD_ORDER)
    values = local_call(
        value_kernel,
        shape((Z, MEMBERS, own_heads * 128)),
        regrouped.reshape(MEMBERS * own_heads, LAT),
        value_blocks,
    )
    right, left = ([(i, (i + step) % X) for i in range(X)] for step in (1, X - 1))
    near = lax.ppermute(payload, "x", right)
    across = lax.ppermute(payload, "x", [(i, (i + 2) % X) for i in range(X)])
    payloads = [across, near, lax.ppermute(payload, "x", left)]
    gathered = exchange(values, "z", z_order(VALUE_FIRST))
    projected = local_call(
        project_kernel,
        shape((MEMBERS, 32, 128)),
        gathered.reshape(Z * MEMBERS, own_heads * 128),
        output_weight,
        *payloads,
    )
    residual_tile = local_call(
        residual_kernel, shape((32, 128), F32), residual, *payloads
    )
    head_parts = exchange(projected, ("role", "tp"), HEAD_ORDER)
    hidden = local_call(hidden_kernel, shape((Z, 32, 128)), head_parts, residual_tile)

    gain_rows = norm_gain.reshape(TP, 1, PLANE)
    own_expert = (gate_weight[0], up_weight[0], down_weight[0])
    peer_expert = [lax.ppermute(weight, "role", swap) for weight in own_expert]
    hidden = exchange(hidden, "z", z_order(HIDDEN_FIRST))
    outbound = local_call(
        dispatch_kernel, shape((X * TP, MOST, PLANE)), hidden, pick
    )
    arrived = exchange(outbound, ("x", "tp"), PLANE_ORDER)
    partial = local_call(
        expert_kernel,
        shape((X * TP, MOST, PLANE)),
        arrived,
        gain_rows,
        slots,
        *own_expert,
        *peer_expert,
    )
    hidden_parts = exchange(partial, ("x", "tp"), PLANE_ORDER)
    columns = local_call(columns_kernel, shape((Z, 32, 128)), hidden_parts)
    returned = exchange(columns, "z", z_order(RETURN_FIRST))
    return local_call(
        combine_kernel,
        shape((COLS, ROWBLK)),
        returned.reshape(Z * 32, 128),
        places,
    )


def solution(mesh):
    grp = ("x", "z")
    fine = Mesh(mesh.devices.reshape(ROLE, X, Z, TP), ("role", "x", "z", "tp"))
    return jax.shard_map(
        shards,
        mesh=fine,
        in_specs=(
            P(("role",) + grp + ("tp",), None, None),
            P(("role",) + grp + ("tp",), None, None),
            P(("role",) + grp + ("tp",)),
            P(("role", "tp"), None, None),
            P(grp, ("role", "tp")),
            P(grp, None),
            P(),
            P(),
            P(),
            P(grp, None, ("role", "tp")),
            P(grp, None, ("role", "tp")),
            P(grp, ("role", "tp"), None),
        ),
        out_specs=P(grp, ("role", "tp")),
        check_vma=False,
    )
```

```python
import jax
import jax.numpy as jnp
from jax import lax
from jax.experimental import pallas as pl
from jax.experimental.pallas import tpu as pltpu
from jax.sharding import Mesh
from jax.sharding import PartitionSpec as P

LAT = 512
SOFTMAX_SCALE = 192.0 ** (-0.5)
NORM_EPS = 1e-06

ROLE, X, Z, TP = 2, 4, 16, 4
MEMBERS = ROLE * TP
ROWBLK = 64
MOST = 16
EXPERTS = 64
COLS = 56
WIDTH = 3584
PLANE = Z * COLS
HALF = 64

VALUE_FIRST, HIDDEN_FIRST, RETURN_FIRST = 8, 4, 8
HEAD_ROLE_FIRST, HEAD_TP_FIRST = 1, 2
PLANE_X_FIRST, PLANE_TP_FIRST = 2, 2


def z_order(first):
    return [(i + first) % Z for i in range(Z)]


def z_places(first):
    return [(z - first) % Z for z in range(Z)]


HEAD_ORDER = [
    (role + HEAD_ROLE_FIRST) % ROLE * TP + (lane + HEAD_TP_FIRST) % TP
    for role in range(ROLE)
    for lane in range(TP)
]
PLANE_ORDER = [
    (x + PLANE_X_FIRST) % X * TP + (lane + PLANE_TP_FIRST) % TP
    for x in range(X)
    for lane in range(TP)
]
HEAD_AT = [HEAD_ORDER.index(i) for i in range(MEMBERS)]
PLANE_AT = [[PLANE_ORDER.index(x * TP + lane) for lane in range(TP)] for x in range(X)]

F32 = jnp.float32
BF16 = jnp.bfloat16
VMEM_LIMIT = 16 * 1024 * 1024
ALL_VMEM = 60 * 1024 * 1024


def nt_dot(a, b):
    return lax.dot_general(a, b, (((1,), (1,)), ((), ())), preferred_element_type=F32)


def nn_dot(a, b):
    return lax.dot_general(a, b, (((1,), (0,)), ((), ())), preferred_element_type=F32)


def local_call(
    body, out_shape, *args, scratch=(), smem=(), hbm=(), out_hbm=(), vmem=VMEM_LIMIT
):
    def space(i, smem, hbm):
        return pltpu.SMEM if i in smem else pltpu.HBM if i in hbm else pltpu.VMEM

    many = isinstance(out_shape, tuple)
    outs = [
        pl.BlockSpec(memory_space=space(i, (), out_hbm))
        for i in range(len(out_shape) if many else 1)
    ]
    return pl.pallas_call(
        body,
        out_shape=out_shape,
        in_specs=[pl.BlockSpec(memory_space=space(i, smem, hbm)) for i in range(len(args))],
        out_specs=tuple(outs) if many else outs[0],
        scratch_shapes=list(scratch),
        compiler_params=pltpu.CompilerParams(vmem_limit_bytes=vmem),
    )(*args)


def exchange(chunks, axes, order):
    return lax.all_to_all(chunks, axes, 0, 0, tiled=True, axis_index_groups=[order])


def whole(dims):
    return pl.BlockSpec(dims, lambda i: (0,) * len(dims))


def shape(dims, dtype=BF16):
    return jax.ShapeDtypeStruct(dims, dtype)


def attend_kernel(
    length_ref, query_ref, cache_ref, weight_ref, residual_ref, out_ref, payload_ref
):
    depth = weight_ref.shape[1]
    span = residual_ref.shape[1] // ROLE
    start = pl.multiple_of(lax.axis_index("role") * span, span)
    payload_ref[:, :depth] = weight_ref[...]
    payload_ref[:, depth:] = residual_ref[:, pl.ds(start, span)]
    cache = cache_ref[0]
    scores = nn_dot(query_ref[0], cache) * SOFTMAX_SCALE
    visible = lax.broadcasted_iota(jnp.int32, scores.shape, 1) < length_ref[0]
    scores = jnp.where(visible, scores, -1e30)
    row_max = jnp.max(scores, axis=1, keepdims=True)
    weights = jnp.where(visible, jnp.exp(scores - row_max), 0.0)
    row_total = jnp.sum(weights, axis=1, keepdims=True)
    summed = nt_dot(weights.astype(BF16), cache[:LAT])
    attended = summed / row_total
    heads = attended.shape[0] // MEMBERS
    attended = [attended[i * heads : (i + 1) * heads] for i in HEAD_ORDER]
    out_ref[...] = jnp.concatenate(attended, axis=0).astype(BF16)


def value_kernel(att_ref, value_ref, out_ref):
    heads = value_ref.shape[0]
    att = att_ref[...]
    rows = att.shape[0]
    row_head = lax.broadcasted_iota(jnp.int32, (rows, 512), 0) % heads
    lane_head = lax.broadcasted_iota(jnp.int32, (rows, 512), 1) // 128
    for head in range(0, heads, 4):
        pair = jnp.concatenate([value_ref[head + i] for i in range(4)], axis=1)
        kept = jnp.where(row_head == head + lane_head, nn_dot(att, pair), 0.0)
        value = jnp.sum(kept.reshape(rows // heads, heads, 512), axis=1)
        value = jnp.concatenate([value[i : i + 1] for i in HEAD_AT], axis=0).astype(BF16)
        out_ref[:, :, head * 128 : (head + 4) * 128] = jnp.broadcast_to(
            value[None], (out_ref.shape[0],) + value.shape
        )


def packed(tile):
    gap = jnp.zeros((ROWBLK // 2, HALF - COLS), F32)
    return jnp.concatenate([tile[: ROWBLK // 2], gap, tile[ROWBLK // 2 :], gap], axis=1)


def by_source(refs):
    for step, ref in zip((0, 2, 3, 1), refs):
        yield lax.rem(lax.axis_index("x") + step, X), ref


def project_kernel(values_ref, *refs):
    weights, out_ref = refs[:X], refs[X]
    depth = values_ref.shape[1]
    values = values_ref[...]
    for x, weight in by_source(weights):
        product = nt_dot(values, weight[:, :depth]).reshape(Z, MEMBERS, COLS)
        lane = lax.rem(x + TP - HEAD_TP_FIRST, TP)
        for role in range(ROLE):
            tile = jnp.concatenate(
                [product[at, role * TP : (role + 1) * TP] for at in z_places(VALUE_FIRST)], axis=0
            )
            out_ref[(role + HEAD_ROLE_FIRST) % ROLE * TP + lane] = packed(tile).astype(BF16)


def residual_kernel(own_ref, *refs):
    payloads, out_ref = refs[: X - 1], refs[X - 1]
    span = ROWBLK * X
    token = lax.broadcasted_iota(jnp.int32, (ROWBLK, span), 0)
    request = lax.broadcasted_iota(jnp.int32, (ROWBLK, span), 1)
    mine = request == token + lax.axis_index("x") * ROWBLK
    start = pl.multiple_of(lax.axis_index("role") * span, span)
    columns = [own_ref[:, pl.ds(start, span)]]
    columns += [payload[:, payload.shape[1] - span :] for payload in payloads]
    total = jnp.zeros((ROWBLK, COLS), F32)
    for x, column in by_source(columns):
        wanted = mine & (x == lax.axis_index("tp"))
        total = total + nt_dot(jnp.where(wanted, 1.0, 0.0).astype(BF16), column)
    out_ref[...] = packed(total)


def hidden_kernel(parts_ref, residual_ref, out_ref):
    total = jnp.sum(parts_ref[...].astype(F32), axis=0)
    total = (residual_ref[...] + total).astype(BF16)
    out_ref[...] = jnp.broadcast_to(total[None], out_ref.shape)


def block_of(ref, block):
    pair = ref[:, pl.ds(pl.multiple_of(block // 2 * (2 * ROWBLK), 2 * ROWBLK), 2 * ROWBLK)]
    return jnp.where(lax.rem(block, 2) == 0, pair[:, :ROWBLK], pair[:, ROWBLK:])


def route_kernel(routed_ref, weight_ref, pick_ref, slots_ref, place_ref, rank_ref):
    role, x, lane = (lax.axis_index(name) for name in ("role", "x", "tp"))
    z = lax.axis_index("z")
    dims = (EXPERTS, ROWBLK)
    expert_ids = lax.broadcasted_iota(jnp.int32, dims, 0)
    earlier = lax.broadcasted_iota(jnp.int32, (ROWBLK, ROWBLK), 0) < lax.broadcasted_iota(
        jnp.int32, (ROWBLK, ROWBLK), 1
    )
    before = jnp.where(earlier, 1.0, 0.0).astype(BF16)
    slots = lax.broadcasted_iota(jnp.int32, (MOST, ROWBLK), 0).astype(F32)

    def ranks(ids):
        named = jnp.zeros(dims, F32)
        for k in range(ids.shape[0]):
            named = named + jnp.where(expert_ids == ids[k : k + 1, :], 1.0, 0.0)
        rank = nn_dot(named.astype(BF16), before)
        return jnp.where(named > 0.5, rank, -1.0)

    rank_ref[...] = ranks(block_of(routed_ref, role * X + x))
    for i in range(X):
        row = rank_ref[pl.ds(i * Z + z, 1), :]
        pick_ref[i * MOST : (i + 1) * MOST, :] = jnp.where(row == slots, 1.0, 0.0).astype(BF16)

    rank_ref[...] = ranks(block_of(routed_ref, role * TP + lane))
    for half in range(2):
        for i in range(Z):
            for pair in range(2):
                expert = (half * 2 + pair) * Z + i
                hit = rank_ref[expert : expert + 1, :] == slots
                rows = pl.ds(z_places(RETURN_FIRST)[i] * 32 + pair * MOST, MOST)
                lanes = pl.ds(half * HALF, ROWBLK)
                place_ref[rows, lanes] = jnp.where(hit, 1.0, 0.0).astype(BF16)

    span = ROWBLK * X
    start = pl.multiple_of(role * span, span)
    mine = routed_ref[:, pl.ds(start, span)] == x * Z + z
    named = jnp.where(mine, 1.0, 0.0)
    weights = jnp.sum(jnp.where(mine, weight_ref[:, pl.ds(start, span)], 0.0), axis=0, keepdims=True)
    source = lax.broadcasted_iota(jnp.int32, (span, span), 0)
    request = lax.broadcasted_iota(jnp.int32, (span, span), 1)
    inside = (source < request) & (source // ROWBLK == request // ROWBLK)
    rank = nn_dot(named.astype(BF16), jnp.where(inside, 1.0, 0.0).astype(BF16))
    rank = jnp.sum(rank, axis=0, keepdims=True)
    chosen = jnp.sum(named, axis=0, keepdims=True)
    rank = jnp.where(chosen > 0.5, rank, -1.0)
    slot = lax.broadcasted_iota(jnp.int32, (X * MOST, span), 0)
    token = lax.broadcasted_iota(jnp.int32, (X * MOST, span), 1)
    hit = (rank == lax.rem(slot, MOST).astype(F32)) & (token // ROWBLK == slot // MOST)
    weight = jnp.sum(jnp.where(hit, weights, 0.0), axis=1, keepdims=True)
    first = jnp.sum(jnp.where(hit, named[:1], 0.0), axis=1, keepdims=True)
    column = lax.broadcasted_iota(jnp.int32, slots_ref.shape, 1)
    slots_ref[...] = jnp.where(column == 0, weight, first)


def dispatch_kernel(parts_ref, pick_ref, out_ref):
    parts = [parts_ref[at].astype(F32) for at in z_places(HIDDEN_FIRST)]
    hidden = jnp.concatenate(
        [
            jnp.concatenate([part[:, start : start + COLS] for part in parts], axis=1)
            for start in (0, HALF)
        ],
        axis=0,
    ).astype(BF16)
    rows = nn_dot(pick_ref[...], hidden).astype(BF16)
    for x in range(X):
        piece = rows[x * MOST : (x + 1) * MOST]
        for lane in range(TP):
            out_ref[PLANE_AT[x][lane]] = piece


def expert_kernel(arrived_ref, gain_ref, slots_ref, *refs):
    own_refs, peer_refs, out_ref = refs[:3], refs[3:6], refs[6]
    rows = X * MOST
    total = jnp.zeros((rows, 1), F32)
    values, scaled = [], []
    for lane in range(TP):
        value = jnp.concatenate(
            [arrived_ref[PLANE_AT[x][lane]] for x in range(X)], axis=0
        ).astype(F32)
        total = total + jnp.sum(value * value, axis=1, keepdims=True)
        values.append(value)
        scaled.append((value * gain_ref[lane]).astype(BF16))

    def hidden_sums(refs):
        sums = jnp.zeros((rows, 256), F32)
        for lane in range(TP):
            depth = pl.ds(lane * PLANE, PLANE)
            both = jnp.concatenate([refs[0][depth], refs[1][depth]], axis=1)
            sums = sums + nn_dot(scaled[lane], both)
        return sums

    own, peer = hidden_sums(own_refs), hidden_sums(peer_refs)
    inverse = lax.rsqrt(total / WIDTH + NORM_EPS)

    def activate(both):
        both = both * inverse
        gate, up = both[:, :128], both[:, 128:]
        return (gate / (1.0 + jnp.exp(-gate)) * up).astype(BF16)

    activated = jnp.concatenate([activate(own), activate(peer)], axis=1)
    weight = slots_ref[:, 0:1]
    first = slots_ref[:, 1:2] * jnp.where(lax.axis_index("tp") == 0, 1.0, 0.0)
    for x in range(X):
        lanes = slice(x * PLANE, (x + 1) * PLANE)
        down = jnp.concatenate([own_refs[2][:, lanes], peer_refs[2][:, lanes]], axis=0)
        product = (nn_dot(activated, down) * weight + values[x] * first).astype(BF16)
        for lane in range(TP):
            out_ref[PLANE_AT[x][lane]] = product[lane * MOST : (lane + 1) * MOST]


def columns_kernel(parts_ref, out_ref):
    summed = []
    for x in range(X):
        total = parts_ref[PLANE_AT[x][0]].astype(F32)
        for lane in range(1, TP):
            total = total + parts_ref[PLANE_AT[x][lane]].astype(F32)
        summed.append(total)
    low = jnp.concatenate(summed[:2], axis=0)
    high = jnp.concatenate(summed[2:], axis=0)
    gap = jnp.zeros((32, HALF - COLS), F32)
    for z in range(Z):
        cut = slice(z * COLS, (z + 1) * COLS)
        out_ref[z_places(RETURN_FIRST)[z]] = jnp.concatenate([low[:, cut], gap, high[:, cut], gap], axis=1).astype(BF16)


def combine_kernel(returned_ref, place_ref, out_ref):
    dims = (((0,), (0,)), ((), ()))
    mixed = lax.dot_general(
        returned_ref[...], place_ref[...], dims, preferred_element_type=F32
    )
    mixed = mixed[:COLS, :ROWBLK] + mixed[HALF : HALF + COLS, HALF : HALF + ROWBLK]
    out_ref[...] = mixed.astype(BF16)


def preload_kernel(*refs):
    count = (len(refs) - 1) // 2
    sems = refs[-1]
    copies = [
        pltpu.make_async_copy(refs[i], refs[count + i], sems.at[i]) for i in range(count)
    ]
    for copy in copies:
        copy.start()
    for copy in copies:
        copy.wait()


def preload(*arrays):
    return local_call(
        preload_kernel,
        tuple(shape(array.shape, array.dtype) for array in arrays),
        *arrays,
        scratch=(pltpu.SemaphoreType.DMA((len(arrays),)),),
        hbm=range(len(arrays)),
    )


def shards(
    queries,
    latent_cache,
    lengths,
    value_up,
    output_weight,
    residual,
    norm_gain,
    routed_experts,
    route_weights,
    gate_weight,
    up_weight,
    down_weight,
):
    swap = [(0, 1), (1, 0)]
    pick, slots, places = local_call(
        route_kernel,
        (shape((X * MOST, ROWBLK)), shape((X * MOST, 128), F32), shape((Z * 32, 128))),
        routed_experts.T,
        route_weights.T,
        scratch=(pltpu.VMEM((EXPERTS, ROWBLK), F32),),
    )

    heads = queries.shape[1]
    own_heads = heads // MEMBERS
    width = output_weight.shape[1] + residual.shape[1] // ROLE
    cache = latent_cache.swapaxes(1, 2)
    attended, payload = pl.pallas_call(
        attend_kernel,
        grid=(1,),
        out_shape=(shape((heads, LAT)), shape((COLS, width))),
        in_specs=[pl.BlockSpec(memory_space=pltpu.SMEM)]
        + [whole(array.shape) for array in (queries, cache, output_weight, residual)],
        out_specs=(whole((heads, LAT)), whole((COLS, width))),
        compiler_params=pltpu.CompilerParams(vmem_limit_bytes=ALL_VMEM),
    )(lengths, queries, cache, output_weight, residual)
    attended, late_value = lax.optimization_barrier((attended, value_up))
    (value_blocks,) = preload(late_value)
    attended = attended.reshape(MEMBERS, own_heads, LAT)
    regrouped = exchange(attended, ("role", "tp"), HEAD_ORDER)
    values = local_call(
        value_kernel,
        shape((Z, MEMBERS, own_heads * 128)),
        regrouped.reshape(MEMBERS * own_heads, LAT),
        value_blocks,
    )
    right, left = ([(i, (i + step) % X) for i in range(X)] for step in (1, X - 1))
    near = lax.ppermute(payload, "x", right)
    across = lax.ppermute(payload, "x", [(i, (i + 2) % X) for i in range(X)])
    payloads = [across, near, lax.ppermute(payload, "x", left)]
    gathered = exchange(values, "z", z_order(VALUE_FIRST))
    projected = local_call(
        project_kernel,
        shape((MEMBERS, 32, 128)),
        gathered.reshape(Z * MEMBERS, own_heads * 128),
        output_weight,
        *payloads,
    )
    residual_tile = local_call(
        residual_kernel, shape((32, 128), F32), residual, *payloads
    )
    head_parts = exchange(projected, ("role", "tp"), HEAD_ORDER)
    hidden = local_call(hidden_kernel, shape((Z, 32, 128)), head_parts, residual_tile)

    gain_rows = norm_gain.reshape(TP, 1, PLANE)
    own_expert = (gate_weight[0], up_weight[0], down_weight[0])
    peer_expert = [lax.ppermute(weight, "role", swap) for weight in own_expert]
    hidden = exchange(hidden, "z", z_order(HIDDEN_FIRST))
    outbound = local_call(
        dispatch_kernel, shape((X * TP, MOST, PLANE)), hidden, pick
    )
    arrived = exchange(outbound, ("x", "tp"), PLANE_ORDER)
    partial = local_call(
        expert_kernel,
        shape((X * TP, MOST, PLANE)),
        arrived,
        gain_rows,
        slots,
        *own_expert,
        *peer_expert,
    )
    hidden_parts = exchange(partial, ("x", "tp"), PLANE_ORDER)
    columns = local_call(columns_kernel, shape((Z, 32, 128)), hidden_parts)
    returned = exchange(columns, "z", z_order(RETURN_FIRST))
    return local_call(
        combine_kernel,
        shape((COLS, ROWBLK)),
        returned.reshape(Z * 32, 128),
        places,
    )


def solution(mesh):
    grp = ("x", "z")
    fine = Mesh(mesh.devices.reshape(ROLE, X, Z, TP), ("role", "x", "z", "tp"))
    return jax.shard_map(
        shards,
        mesh=fine,
        in_specs=(
            P(("role",) + grp + ("tp",), None, None),
            P(("role",) + grp + ("tp",), None, None),
            P(("role",) + grp + ("tp",)),
            P(("role", "tp"), None, None),
            P(grp, ("role", "tp")),
            P(grp, None),
            P(),
            P(),
            P(),
            P(grp, None, ("role", "tp")),
            P(grp, None, ("role", "tp")),
            P(grp, ("role", "tp"), None),
        ),
        out_specs=P(grp, ("role", "tp")),
        check_vma=False,
    )
```
